256 devices in a mesh: gx: 16 (over y_hi, x, core), gy: 16 (over z, y_lo).
Axes of the slice: x: 4, y: 4 (y_hi: 2, y_lo: 2; y = y_hi * 2 + y_lo), z: 8, core: 2. Of those that a mesh axis runs over, the one named last changes fastest.
Arguments:
- state: float32 [9, 4, 256, 2048], P(None, None, 'gy', 'gx'), may hold values from -3 to 11, as said below
- inflow: float32 [9, 4, 256, 8], P(None, None, 'gy'), may hold values from -3 to 11, as said below
Outputs:
- advanced: float32 [9, 4, 256, 2048], P(None, None, 'gy', 'gx')
The draws below stay inside these ranges and needn't reach their ends.
Inputs may be any that keep to these rules, and one draw needn't show every extreme that they name: Every cell is a physical state: density and pressure between 0.5 and 1.8, each species density between 0 and the density. `inflow`: every cell is a physical state: density and pressure between 0.5 and 1.8, each species density between 0 and the density.
All inputs are finite; a program needn't handle non-finite values.
Results may differ from the reference program's by a relative error of at most 0.00002.
Values sent between devices are 32-bit elements; how exact they have to be, the bound alone decides.
A program may use at most 64 MiB of HBM per device.

```python
import math
import jax
import jax.numpy as jnp
from jax import lax

CX = 128
NZ = 4
SHIFT = 8
SUBSTEPS = 4
NX = 2048
NY = 256


def build_state(key, position, spread, tail, bump):
    count = position.shape[0]
    shape = (NZ, NY, count)
    keys = jax.random.split(key, 9)
    along = position[None, None, :]
    density = jax.random.uniform(keys[0], shape, jnp.float32, 0.7, 1.4) * (1.0 + bump * jnp.sin(2.0 * math.pi * along))
    press = jax.random.uniform(keys[1], shape, jnp.float32, 0.7, 1.4) * (1.0 + bump * jnp.cos(2.0 * math.pi * along))
    velocity = [jax.random.truncated_normal(keys[2 + index], -tail, tail, shape, jnp.float32) * spread for index in range(3)]
    fractions = [jax.random.uniform(keys[5], shape, jnp.float32, 0.2, 0.8)]
    fractions = fractions + [jax.random.uniform(keys[6 + index], shape, jnp.float32, 0.0, 0.5) for index in range(3)]
    kinetic = 0.5 * density * (velocity[0] ** 2 + velocity[1] ** 2 + velocity[2] ** 2)
    energy = press / 0.4 + kinetic + density * fractions[0]
    parts = [density] + [density * item for item in velocity] + [energy] + [density * item for item in fractions]
    return jnp.stack(parts).astype(jnp.float32)


def fast_region(key):
    place = jax.random.uniform(jax.random.fold_in(key, 5), (2,), jnp.float32, 0.0, 1.0)
    centre_x = 0.1 + 0.6 * place[0]
    centre_y = place[1]
    position = jnp.arange(NX, dtype=jnp.float32) / NX
    across = jnp.arange(NY, dtype=jnp.float32) / NY
    reach_x = jnp.exp(-0.5 * ((position - centre_x) / 0.08) ** 2)
    reach_y = jnp.exp((jnp.cos(2.0 * math.pi * (across - centre_y)) - 1.0) / (4.0 * math.pi * math.pi * 0.01))
    return 0.15 + 0.3 * reach_y[None, :, None] * reach_x[None, None, :]


def draw_state(key, part):
    key = jax.random.fold_in(key, 11)
    position = jnp.arange(NX, dtype=jnp.float32) / NX
    spread = fast_region(key)
    return build_state(key, position, spread, 3.0, 0.0)


def draw_inflow(key, part):
    key = jax.random.fold_in(key, 23)
    position = jnp.ones((SHIFT,), jnp.float32)
    spread = jnp.full((1, NY, SHIFT), 0.15, jnp.float32)
    return build_state(key, position, spread, 3.0, 0.0)


def setup_inputs(seed: int = 0) -> dict:
    streams_of = jax.random.split(jax.random.key(seed), 3)
    state = draw_state(jax.random.fold_in(streams_of[2], 71), 0)
    inflow = draw_inflow(jax.random.fold_in(streams_of[2], 71), 0)
    return {"state": state, "inflow": inflow}


GAMMA = 1.4
HEAT = 1.0
PREFACTOR = 300.0
ACTIVATION = 4.0
COURANT = 0.15
WENO_EPS = 1e-06

def pressure(state):
    density = state[0]
    kinetic = 0.5 * (state[1] * state[1] + state[2] * state[2] + state[3] * state[3]) / density
    return (GAMMA - 1.0) * (state[4] - kinetic - HEAT * state[5])

def wave_speed(state):
    density = state[0]
    sound = jnp.sqrt(GAMMA * pressure(state) / density)
    fastest = jnp.maximum(jnp.maximum(jnp.abs(state[1]), jnp.abs(state[2])), jnp.abs(state[3])) / density
    return jnp.max(fastest + sound)

def flux(state, component):
    velocity = state[component] / state[0]
    press = pressure(state)
    moved = [velocity * state[index] for index in range(9)]
    moved[component] = moved[component] + press
    moved[4] = moved[4] + velocity * press
    return jnp.stack(moved)

def weno(far_left, near_left, centre, near_right, far_right):
    smooth_zero = 13.0 / 12.0 * (far_left - 2.0 * near_left + centre) ** 2 + 0.25 * (far_left - 4.0 * near_left + 3.0 * centre) ** 2
    smooth_one = 13.0 / 12.0 * (near_left - 2.0 * centre + near_right) ** 2 + 0.25 * (near_left - near_right) ** 2
    smooth_two = 13.0 / 12.0 * (centre - 2.0 * near_right + far_right) ** 2 + 0.25 * (3.0 * centre - 4.0 * near_right + far_right) ** 2
    weight_zero = 0.1 / (WENO_EPS + smooth_zero) ** 2
    weight_one = 0.6 / (WENO_EPS + smooth_one) ** 2
    weight_two = 0.3 / (WENO_EPS + smooth_two) ** 2
    guess_zero = (2.0 * far_left - 7.0 * near_left + 11.0 * centre) / 6.0
    guess_one = (-near_left + 5.0 * centre + 2.0 * near_right) / 6.0
    guess_two = (2.0 * centre + 5.0 * near_right - far_right) / 6.0
    return (weight_zero * guess_zero + weight_one * guess_one + weight_two * guess_two) / (weight_zero + weight_one + weight_two)

def interface_sum(plus, minus, axis, count):

    def part(array, start):
        return lax.slice_in_dim(array, start, start + count + 1, axis=axis)
    faces = weno(part(plus, 0), part(plus, 1), part(plus, 2), part(plus, 3), part(plus, 4))
    faces = faces + weno(part(minus, 5), part(minus, 4), part(minus, 3), part(minus, 2), part(minus, 1))
    return lax.slice_in_dim(faces, 1, count + 1, axis=axis) - lax.slice_in_dim(faces, 0, count, axis=axis)

def directional(block, component, axis, speed):
    count = block.shape[axis] - 6
    read = flux(block, component)
    plus = 0.5 * (read + speed * block)
    minus = 0.5 * (read - speed * block)
    return interface_sum(plus, minus, axis, count)

def rates(padded, speed):
    rows = padded[:, :, 3:-3, :]
    columns = padded[:, :, :, 3:-3]
    core = padded[:, :, 3:-3, 3:-3]
    layers = jnp.concatenate([core[:, -3:], core, core[:, :3]], axis=1)
    total = directional(rows, 1, 3, speed) + directional(columns, 2, 2, speed) + directional(layers, 3, 1, speed)
    return -total

def react(state, step):
    small = step / SUBSTEPS
    for substep in range(SUBSTEPS):
        temper = pressure(state) / state[0]
        burned = small * PREFACTOR * state[5] * jnp.exp(-ACTIVATION / temper)
        state = jnp.concatenate([state[:5], (state[5] - burned)[None], (state[6] + burned)[None], state[7:]], axis=0)
    return state

def field_rates(state, speed):
    padded = jnp.pad(state, ((0, 0), (0, 0), (3, 3), (0, 0)), mode='wrap')
    padded = jnp.pad(padded, ((0, 0), (0, 0), (0, 0), (3, 3)), mode='edge')
    width = math.gcd(CX, 32)
    blocks = NX // width

    def one_block(index):
        piece = lax.dynamic_slice_in_dim(padded, index * width, width + 6, axis=3)
        return rates(piece, speed)
    result = lax.map(one_block, jnp.arange(blocks, dtype=jnp.int32))
    return jnp.moveaxis(result, 0, 3).reshape(9, NZ, NY, NX)

def reference(state, inflow):
    shifted = jnp.concatenate([state[..., SHIFT:], inflow], axis=3)
    speed = wave_speed(shifted)
    step = COURANT / speed
    first = shifted + step * field_rates(shifted, speed)
    second = 0.75 * shifted + 0.25 * (first + step * field_rates(first, speed))
    third = shifted / 3.0 + 2.0 / 3.0 * (second + step * field_rates(second, speed))
    return react(third, step)
```

```python
import functools

import jax
import jax.numpy as jnp
from jax import lax
from jax.experimental import pallas as pl
from jax.experimental.pallas import tpu as pltpu
from jax.sharding import PartitionSpec as P

MESH = pl.DeviceIdType.MESH
NZ = 4
NY = 16
LANES = 128
COMPS = 9
GROUPS = 8
BLOCKS = 9
SUBSTEPS = 4
PREFACTOR = 300.0
ACTIVATION = 4.0
COURANT = 0.15
EPS = 3e-6
STAGES = ((0.0, 1.0), (0.75, 0.25), (1.0 / 3.0, 2.0 / 3.0))


def reciprocal(x):
    return pltpu.reciprocal(x, approx=True)


def roll(x, shift):
    shift = shift % LANES
    return x if shift == 0 else pltpu.roll(x, shift, axis=1)


def cell_terms(d_low, d_high, q_low, q_high):
    second = d_high - d_low
    cross = d_high * d_low
    squares = (q_low + q_high) + EPS
    base = squares - 2.75 * cross
    r_low = reciprocal(base + 1.5 * q_high)
    r_mid = reciprocal(squares - 1.25 * cross)
    r_high = reciprocal(base + 1.5 * q_low)
    return second, r_low * r_low, 6.0 * (r_mid * r_mid), r_high * r_high


def correction(w_far, w_mid, w_near, t_far, t_near):
    near = 3.0 * w_near
    return (w_far * t_far + near * (0.5 * t_near)) * reciprocal((w_far + w_mid) + near)


def plus_face(g, d_low, d_high, fix):
    return 6.0 * g + d_low + 2.0 * (d_high - fix)


def minus_face(g, d_low, d_high, fix):
    return 6.0 * g - d_high - 2.0 * (d_low - fix)


def stream_faces(load, first, last, emit):
    gp, gm, dp, dm, qp, qm = {}, {}, {}, {}, {}, {}
    tp, tm, sp, sm, wp, wm = {}, {}, {}, {}, {}, {}
    plus = {}
    for j in range(first - 2, last + 4):
        gp[j], gm[j] = load(j)
        k = j - 1
        if j > first - 2:
            dp[k] = gp[j] - gp[k]
            qp[k] = dp[k] * dp[k]
            dm[k] = gm[j] - gm[k]
            qm[k] = dm[k] * dm[k]
        if j >= first:
            sp[k], *wp[k] = cell_terms(dp[k - 1], dp[k], qp[k - 1], qp[k])
            sm[k], *wm[k] = cell_terms(dm[k - 1], dm[k], qm[k - 1], qm[k])
            if k > first - 1:
                tp[k - 1] = sp[k] - sp[k - 1]
                tm[k - 1] = sm[k] - sm[k - 1]
            i = k - 1
            if first <= i <= last:
                fix = correction(wp[i - 1][0], wp[i][1], wp[i + 1][2], tp[i - 1], tp[i])
                plus[i] = plus_face(gp[i], dp[i - 1], dp[i], fix)
            i, c = k - 2, k - 1
            if first <= i <= last:
                fix = correction(wm[c + 1][2], wm[c][1], wm[c - 1][0], tm[c], tm[c - 1])
                emit(i, plus[i] + minus_face(gm[c], dm[c - 1], dm[c], fix))


def ring_differences(gp, gm):
    n = len(gp)

    def up(x):
        return [x[(i + 1) % n] for i in range(n)]

    def down(x):
        return [x[(i - 1) % n] for i in range(n)]

    def parts(g):
        d = [b - a for a, b in zip(g, up(g))]
        q = [a * a for a in d]
        terms = [cell_terms(*each) for each in zip(down(d), d, down(q), q)]
        s, low, mid, high = map(list, zip(*terms))
        t = [b - a for a, b in zip(s, up(s))]
        return d, t, low, mid, high

    d, t, low, mid, high = parts(gp)
    fix = [correction(*each) for each in zip(down(low), mid, up(high), down(t), t)]
    plus = [plus_face(*each) for each in zip(gp, down(d), d, fix)]
    d, t, low, mid, high = parts(gm)
    fix = [correction(*each) for each in zip(up(high), mid, down(low), t, down(t))]
    minus = [minus_face(*each) for each in zip(gm, down(d), d, fix)]
    faces = [a + b for a, b in zip(plus, up(minus))]
    return [a - b for a, b in zip(faces, down(faces))]


def lane_faces(gp, gm):
    def up(x):
        return roll(x, -1)

    def down(x):
        return roll(x, 1)

    def parts(g):
        d_high = up(g) - g
        d_low = down(d_high)
        second, low, mid, high = cell_terms(d_low, d_high, d_low * d_low, d_high * d_high)
        return d_low, d_high, up(second) - second, second - down(second), down(low), mid, up(high)

    d_low, d_high, t_up, t_down, low, mid, high = parts(gp)
    plus = plus_face(gp, d_low, d_high, correction(low, mid, high, t_down, t_up))
    d_low, d_high, t_up, t_down, low, mid, high = parts(gm)
    minus = minus_face(gm, d_low, d_high, correction(high, mid, low, t_up, t_down))
    return plus + up(minus)


def primitives(rho, m1, m2, m3, energy, reactant):
    inverse = reciprocal(rho)
    v1, v2, v3 = m1 * inverse, m2 * inverse, m3 * inverse
    kinetic = 0.5 * (m1 * v1 + m2 * v2 + m3 * v3)
    return v1, v2, v3, 0.4 * (energy - kinetic - reactant)


def signal_speed(rho, m1, m2, m3, energy, reactant):
    press = primitives(rho, m1, m2, m3, energy, reactant)[3]
    inverse = reciprocal(rho)
    fastest = jnp.maximum(jnp.maximum(jnp.abs(m1), jnp.abs(m2)), jnp.abs(m3))
    return fastest * inverse + jnp.sqrt(1.4 * press * inverse)


def kernel(
    nx, ny, state, inflow, out,
    raw, infl, result, fields, cells, prim, halo_prim, flux_p, flux_m, acc, faces,
    windows, edges, ninth_p, ninth_m, ninth_d, pack, from_left, from_right, halo, peak_x, peak_y, consts,
    local_sem, send_sem, recv_sem,
):
    me_x, me_y = lax.axis_index("gx"), lax.axis_index("gy")
    is_first, is_last = me_x == 0, me_x == nx - 1
    lane = lax.broadcasted_iota(jnp.int32, (8, LANES), 1)
    sub = lax.broadcasted_iota(jnp.int32, (8, LANES), 0)
    place = lane & 15

    def peer(dx, dy):
        return (lax.rem(me_x + (dx + nx), nx), lax.rem(me_y + (dy + ny), ny))

    def remote(src, dst, slot, target):
        return pltpu.make_async_remote_copy(
            src_ref=src, dst_ref=dst, send_sem=send_sem.at[slot], recv_sem=recv_sem.at[slot],
            device_id=target, device_id_type=MESH,
        )

    fetch_state = pltpu.make_async_copy(state, raw, local_sem.at[0])
    fetch_inflow = pltpu.make_async_copy(inflow, infl, local_sem.at[1])
    fetch_state.start()
    fetch_inflow.start()
    barrier = pltpu.get_barrier_semaphore()
    for k in range(1, nx):
        pl.semaphore_signal(barrier, inc=1, device_id=peer(k, 0), device_id_type=MESH)
    for k in range(1, ny):
        pl.semaphore_signal(barrier, inc=1, device_id=peer(0, k), device_id_type=MESH)
    fetch_state.wait()
    fetch_inflow.wait()

    def tile_speed(ref, g):
        rows = [ref[pl.ds(64 * c + 8 * g, 8), :] for c in range(6)]
        return signal_speed(*rows)

    peak = tile_speed(raw, 0)
    entering = tile_speed(infl, 0)
    for g in range(1, GROUPS):
        peak = jnp.maximum(peak, tile_speed(raw, g))
        entering = jnp.maximum(entering, tile_speed(infl, g))
    peak = jnp.where(is_first & (lane < 8), 0.0, peak)
    peak_x[pl.ds(0, 8), :] = jnp.maximum(peak, jnp.max(entering))

    pl.semaphore_wait(barrier, nx + ny - 2)

    def spread(buffer, count, base, step):
        copies = []
        for k in range(1, count):
            copies.append(
                remote(buffer.at[pl.ds(0, 8)], buffer.at[pl.ds(8 * k, 8)], base + k, peer(*step(k)))
            )
            copies[-1].start()
        return copies

    def gather(buffer, copies):
        total = buffer[pl.ds(0, 8), :]
        for k, copy in enumerate(copies):
            copy.wait_recv()
            total = jnp.maximum(total, buffer[pl.ds(8 * (k + 1), 8), :])
        return total

    sent_x = spread(peak_x, nx, 0, lambda k: (k, 0))

    def pack_opening(q, _):
        head = jnp.zeros((8, LANES), jnp.float32)
        own = head
        for g in range(GROUPS):
            block = opening_block(raw, g, q)
            here = (lane >> 4) == g
            head = jnp.where(here, roll(block, 16 * g + 5), head)
            own = jnp.where(here, roll(block, 16 * g - 5), own)
        pack[0, pl.ds(pl.multiple_of(8 * q, 8), 8), :] = head
        windows[pl.ds(pl.multiple_of(8 * q, 8), 8), :] = own
        return 0

    def opening_block(ref, g, q):
        if isinstance(q, int) and q == 8:
            return ref[pl.ds(64 * 8 + 8 * g, 8), :]
        return ref[pl.ds(8 * g + q, 8, stride=64), :]

    lax.fori_loop(0, 8, pack_opening, 0)
    pack_opening(8, 0)

    shift_copy = remote(pack.at[0], from_right.at[0], 2 * 16, peer(-1, 0))

    @pl.when(me_x > 0)
    def _():
        shift_copy.start()

    @pl.when(is_last)
    def _():
        def pack_inflow(q, _):
            head = jnp.zeros((8, LANES), jnp.float32)
            for g in range(GROUPS):
                block = opening_block(infl, g, q)
                block = jnp.concatenate([block, jnp.zeros((8, LANES - 8), jnp.float32)], axis=1)
                head = jnp.where((lane >> 4) == g, roll(block, 16 * g + 5), head)
            for k in range(1, 4):
                head = jnp.where(place == 12 + k, roll(head, k), head)
            from_right[0, pl.ds(pl.multiple_of(8 * q, 8), 8), :] = head
            return 0

        lax.fori_loop(0, 8, pack_inflow, 0)
        pack_inflow(8, 0)

    peak_y[pl.ds(0, 8), :] = gather(peak_x, sent_x)
    sent_y = spread(peak_y, ny, 16, lambda k: (0, k))

    @pl.when(jnp.logical_not(is_last))
    def _():
        shift_copy.wait_recv()

    def assemble(q, _):
        rows = pl.ds(pl.multiple_of(8 * q, 8), 8)
        arrived = from_right[0, rows, :]
        for g in range(GROUPS):
            block = opening_block(raw, g, q)
            block = jnp.where(lane < LANES - 8, roll(block, -8), roll(arrived, 115 - 16 * g))
            fields[0, g // 2, g % 2, rows, :] = block
        own = windows[rows, :]
        edge = own
        for k in range(1, 4):
            edge = jnp.where(place == 3 - k, roll(own, -k), edge)
        own = jnp.where(is_first, edge, own)
        windows[rows, :] = jnp.where(place < 8, own, arrived)
        return 0

    lax.fori_loop(0, 8, assemble, 0)
    assemble(8, 0)

    def y_copies(stage):
        now, base = fields.at[stage], 33 + 3 * stage
        low, high = halo.at[stage, 0], halo.at[stage, 1]
        return [
            remote(now.at[:, 1, 40:72, :], low, base, peer(0, 1)),
            remote(now.at[:, 0, 0:24, :], high.at[:, 0:24, :], base + 1, peer(0, -1)),
            remote(now.at[:, 0, 64:72, :], high.at[:, 24:32, :], base + 2, peer(0, -1)),
        ]

    def x_copies(stage):
        base = 42 + 2 * (stage - 1)
        return [
            remote(pack.at[stage], from_left.at[stage], base, peer(1, 0)),
            remote(pack.at[stage], from_right.at[stage], base + 1, peer(-1, 0)),
        ]

    for copy in y_copies(0):
        copy.start()

    top = jnp.max(gather(peak_y, sent_y))
    speed = jnp.full((8, LANES), top, jnp.float32)
    consts[0] = speed
    consts[1] = COURANT / speed

    def fluxes(block, velocity, press, lam, component):
        flow = velocity * (block + jnp.where(sub == 4, press, 0.0))
        flow = flow + jnp.where(sub == component, press, 0.0)
        move = lam * block
        return flow + move, flow - move

    def ninth_fluxes(block, velocity, lam):
        flow, move = velocity * block, lam * block
        return flow + move, flow - move

    for stage in range(3):
        now = fields.at[stage]
        lam = consts[0]

        def own_primitives(g, _):
            z, t = g // 2, g % 2
            rows = [now[z, t, pl.ds(c, 8, stride=8), :] for c in range(6)]
            for index, value in enumerate(primitives(*rows)):
                prim[index, g] = value
            return 0

        lax.fori_loop(0, GROUPS, own_primitives, 0)

        def spanwise(t, _):
            for q in range(BLOCKS):
                rows = pl.ds(8 * q, 8)
                gp, gm = [], []
                for z in range(NZ):
                    block = now[z, t, rows, :]
                    if q < 8:
                        v1, v3, press = (prim[i, 2 * z + t, q : q + 1, :] for i in (0, 2, 3))
                        one = fluxes(block, v1, press, lam, 1)
                        three = fluxes(block, v3, press, lam, 3)
                    else:
                        one = ninth_fluxes(block, prim[0, 2 * z + t], lam)
                        three = ninth_fluxes(block, prim[2, 2 * z + t], lam)
                    flux_p[z, t, rows, :], flux_m[z, t, rows, :] = one
                    gp.append(three[0])
                    gm.append(three[1])
                for z, value in enumerate(ring_differences(gp, gm)):
                    acc[z, t, rows, :] = value
            return 0

        lax.fori_loop(0, 2, spanwise, 0)

        def streamwise(g, _):
            z, t = g // 2, g % 2
            for q in range(BLOCKS):
                rows = pl.ds(8 * q, 8)
                faces[z, t, rows, :] = lane_faces(flux_p[z, t, rows, :], flux_m[z, t, rows, :])
            return 0

        lax.fori_loop(0, GROUPS, streamwise, 0)

        if stage > 0:
            left, right = x_copies(stage)

            @pl.when(me_x > 0)
            def _():
                left.wait_recv()

            @pl.when(jnp.logical_not(is_last))
            def _():
                right.wait_recv()

            for q in range(BLOCKS):
                rows = pl.ds(8 * q, 8)
                own = pack[stage, rows, :]
                low, high = own, own
                for k in range(1, 4):
                    low = jnp.where(place == 3 - k, roll(own, -k), low)
                    high = jnp.where(place == 12 + k, roll(own, k), high)
                low = jnp.where(is_first, low, from_left[stage, rows, :])
                high = jnp.where(is_last, high, from_right[stage, rows, :])
                windows[rows, :] = jnp.where(place < 3, low, jnp.where(place > 12, high, own))

        rows6 = [windows[pl.ds(c, 8, stride=8), :] for c in range(6)]
        v1, _, _, press = primitives(*rows6)
        edges[0, pl.ds(0, 8), :] = v1
        edges[0, pl.ds(8, 8), :] = press
        for q in range(BLOCKS):
            rows = pl.ds(8 * q, 8)
            block = windows[rows, :]
            if q < 8:
                pair = fluxes(block, edges[0, q : q + 1, :], edges[0, 8 + q : 9 + q, :], lam, 1)
            else:
                pair = ninth_fluxes(block, v1, lam)
            h = lane_faces(*pair)
            edges[1, rows, :] = h
            edges[2, rows, :] = jnp.where(place < 3, roll(h, -10), h)

        for copy in y_copies(stage):
            copy.wait_recv()
        for side in range(2):
            for z in range(NZ):
                rows = [halo[stage, side, z, pl.ds(c, 3, stride=8), :] for c in range(6)]
                _, v2, _, press = primitives(*rows)
                start = 5 if side == 0 else 0
                halo_prim[0, side, z, start : start + 3, :] = v2
                halo_prim[1, side, z, start : start + 3, :] = press

        def transverse(z, _):
            def load(j):
                if 0 <= j < NY:
                    t, q = j // 8, j % 8
                    block = now[z, t, pl.ds(8 * q, 8), :]
                    v2, press = (prim[i, 2 * z + t, q : q + 1, :] for i in (1, 3))
                else:
                    side, q = (0, j + 8) if j < 0 else (1, j - NY)
                    block = halo[stage, side, z, pl.ds(8 * (j + 3 if j < 0 else q), 8), :]
                    v2, press = (halo_prim[i, side, z, q : q + 1, :] for i in (0, 1))
                return fluxes(block, v2, press, lam, 2)

            before = {}

            def emit(i, face):
                before[i] = face
                if i >= 0:
                    rows = pl.ds(8 * (i % 8), 8)
                    acc[z, i // 8, rows, :] += face - before.pop(i - 1)

            stream_faces(load, -1, NY - 1, emit)

            tiles = [
                (halo[stage, 0, z, pl.ds(24, 8), :], halo_prim[0, 0, z]),
                (now[z, 0, pl.ds(64, 8), :], prim[1, 2 * z]),
                (now[z, 1, pl.ds(64, 8), :], prim[1, 2 * z + 1]),
                (halo[stage, 1, z, pl.ds(24, 8), :], halo_prim[0, 1, z]),
            ]
            for index, (block, v2) in enumerate(tiles):
                plus, minus = ninth_fluxes(block, v2, lam)
                for h in range(2):
                    if 0 <= index - h < 3:
                        start = pl.multiple_of(24 * z + 96 * h + 8 * (index - h), 8)
                        ninth_p[pl.ds(start, 8), :] = plus
                        ninth_m[pl.ds(start, 8), :] = minus
            return 0

        lax.fori_loop(0, NZ, transverse, 0)

        before = {}

        def emit_ninth(i, face):
            before[i] = face
            if i >= 0:
                ninth_d[pl.ds(i, 8, stride=8), :] = face - before.pop(i - 1)

        def load_ninth(j):
            rows = pl.ds(8 + j, 8, stride=24)
            return ninth_p[rows, :], ninth_m[rows, :]

        stream_faces(load_ninth, -1, 7, emit_ninth)
        for h in range(2):
            for z in range(NZ):
                acc[z, h, pl.ds(64, 8), :] += ninth_d[pl.ds(8 * (4 * h + z), 8), :]

        keep, blend = STAGES[stage]

        def update(q, _):
            rows = pl.ds(pl.multiple_of(8 * q, 8), 8)
            scale = consts[1] * (blend / 12.0)
            h_low, h_edge = edges[1, rows, :], edges[2, rows, :]
            packed = jnp.zeros((8, LANES), jnp.float32)
            for g in range(GROUPS):
                z, t = g // 2, g % 2
                face = faces[z, t, rows, :]
                face = jnp.where((lane < 2) | (lane > 124), roll(h_edge, -16 * g - 3), face)
                below = jnp.where(lane == 0, roll(h_low, -16 * g - 2), roll(face, 1))
                total = acc[z, t, rows, :] + (face - below)
                value = now[z, t, rows, :]
                if stage > 0:
                    value = keep * fields[0, z, t, rows, :] + blend * value
                value = value - scale * total
                fields[stage + 1, z, t, rows, :] = value
                if stage < 2:
                    here = (lane >> 4) == g
                    ends = jnp.where(place < 8, roll(value, 16 * g + 3), roll(value, 16 * g + 13))
                    packed = jnp.where(here, ends, packed)
            if stage < 2:
                pack[stage + 1, rows, :] = packed
            return 0

        lax.fori_loop(0, BLOCKS, update, 0)

        if stage < 2:
            for copy in y_copies(stage + 1):
                copy.start()
            left, right = x_copies(stage + 1)

            @pl.when(jnp.logical_not(is_last))
            def _():
                left.start()

            @pl.when(me_x > 0)
            def _():
                right.start()

    third = fields.at[3]

    def react(g, _):
        z, t = g // 2, g % 2
        rows = [third[z, t, pl.ds(c, 8, stride=8), :] for c in range(8)]
        rho, m1, m2, m3, energy, reactant, product, other = rows
        inverse = reciprocal(rho)
        rest = energy - 0.5 * (m1 * m1 + m2 * m2 + m3 * m3) * inverse
        small = consts[1] * (PREFACTOR / SUBSTEPS)
        for _ in range(SUBSTEPS):
            press = 0.4 * (rest - reactant)
            burned = small * reactant * jnp.exp(-ACTIVATION * (rho * reciprocal(press)))
            reactant, product = reactant - burned, product + burned
        rows = [rho, m1, m2, m3, energy, reactant, product, other, third[z, t, pl.ds(64, 8), :]]
        for c, value in enumerate(rows):
            result[pl.ds(pl.multiple_of(64 * c + 8 * g, 8), 8), :] = value
        return 0

    lax.fori_loop(0, GROUPS, react, 0)
    deliver = pltpu.make_async_copy(result, out, local_sem.at[0])
    deliver.start()

    for copy in sent_x + sent_y + y_copies(0) + y_copies(1) + y_copies(2):
        copy.wait_send()
    for stage in (1, 2):
        left, right = x_copies(stage)

        @pl.when(jnp.logical_not(is_last))
        def _():
            left.wait_send()

        @pl.when(me_x > 0)
        def _():
            right.wait_send()

    @pl.when(me_x > 0)
    def _():
        shift_copy.wait_send()

    deliver.wait()


def on_device(nx, ny, state, inflow):
    rows = COMPS * NZ * NY
    f32 = jnp.float32

    def vmem(*shape):
        return pltpu.VMEM(shape, f32)

    result = pl.pallas_call(
        functools.partial(kernel, nx, ny),
        out_shape=jax.ShapeDtypeStruct((rows, LANES), f32),
        in_specs=[pl.BlockSpec(memory_space=pl.ANY)] * 2,
        out_specs=pl.BlockSpec(memory_space=pl.ANY),
        scratch_shapes=[
            vmem(rows, LANES),
            vmem(rows, inflow.shape[-1]),
            vmem(rows, LANES),
            vmem(4, NZ, 2, 72, LANES),
            vmem(8, LANES),
            vmem(4, GROUPS, 8, LANES),
            vmem(2, 2, NZ, 8, LANES),
            vmem(NZ, 2, 72, LANES),
            vmem(NZ, 2, 72, LANES),
            vmem(NZ, 2, 72, LANES),
            vmem(NZ, 2, 72, LANES),
            vmem(72, LANES),
            vmem(3, 72, LANES),
            vmem(192, LANES),
            vmem(192, LANES),
            vmem(64, LANES),
            vmem(3, 72, LANES),
            vmem(3, 72, LANES),
            vmem(3, 72, LANES),
            vmem(3, 2, NZ, 32, LANES),
            vmem(8 * 16, LANES),
            vmem(8 * 16, LANES),
            vmem(2, 8, LANES),
            pltpu.SemaphoreType.DMA((2,)),
            pltpu.SemaphoreType.DMA((46,)),
            pltpu.SemaphoreType.DMA((46,)),
        ],
        compiler_params=pltpu.CompilerParams(
            collective_id=0, has_side_effects=True, vmem_limit_bytes=32 * 1024 * 1024
        ),
        cost_estimate=pl.CostEstimate(
            flops=60_000_000, bytes_accessed=1_200_000, transcendentals=5_000_000
        ),
    )(state.reshape(rows, LANES), inflow.reshape(rows, inflow.shape[-1]))
    return result.reshape(state.shape)


def solution(mesh):
    return jax.shard_map(
        functools.partial(on_device, mesh.shape["gx"], mesh.shape["gy"]),
        mesh=mesh,
        in_specs=(P(None, None, "gy", "gx"), P(None, None, "gy", None)),
        out_specs=P(None, None, "gy", "gx"),
        check_vma=False,
    )
```

```python
import functools

import jax
import jax.numpy as jnp
from jax import lax
from jax.experimental import pallas as pl
from jax.experimental.pallas import tpu as pltpu
from jax.sharding import PartitionSpec as P

MESH = pl.DeviceIdType.MESH
NZ = 4
NY = 16
LANES = 128
COMPS = 9
GROUPS = 8
BLOCKS = 9
SUBSTEPS = 4
PREFACTOR = 300.0
ACTIVATION = 4.0
COURANT = 0.15
EPS = 2e-6
STAGES = ((0.0, 1.0), (0.75, 0.25), (1.0 / 3.0, 2.0 / 3.0))


def reciprocal(x):
    return pltpu.reciprocal(x, approx=True)


def roll(x, shift):
    shift = shift % LANES
    return x if shift == 0 else pltpu.roll(x, shift, axis=1)


def cell_terms(d_low, d_high, q_low, q_high):
    second = d_high - d_low
    half = d_low * (0.5 * d_high)
    level = (2.0 / 3.0) * (second * second) + EPS
    base = level - half
    r_low = reciprocal(base + q_high)
    r_mid = reciprocal(level + half)
    r_high = reciprocal(base + q_low)
    return second, r_low * r_low, 6.0 * (r_mid * r_mid), r_high * r_high


def correction(w_far, w_mid, w_near, t_far, t_near):
    near = 3.0 * w_near
    return (w_far * t_far + near * (0.5 * t_near)) * reciprocal((w_far + w_mid) + near)


def face_value(gp, gm, dp_low, dp_high, dm_low, dm_high, fix_p, fix_m):
    inner = (dp_high - dm_low) - (fix_p - fix_m)
    return 6.0 * (gp + gm) + (dp_low - dm_high) + 2.0 * inner


def stream_faces(load, first, last, emit):
    gp, gm, dp, dm, qp, qm = {}, {}, {}, {}, {}, {}
    tp, tm, sp, sm, wp, wm = {}, {}, {}, {}, {}, {}
    fix = {}
    for j in range(first - 2, last + 4):
        gp[j], gm[j] = load(j)
        k = j - 1
        if j > first - 2:
            dp[k] = gp[j] - gp[k]
            qp[k] = dp[k] * dp[k]
            dm[k] = gm[j] - gm[k]
            qm[k] = dm[k] * dm[k]
        if j >= first:
            sp[k], *wp[k] = cell_terms(dp[k - 1], dp[k], qp[k - 1], qp[k])
            sm[k], *wm[k] = cell_terms(dm[k - 1], dm[k], qm[k - 1], qm[k])
            if k > first - 1:
                tp[k - 1] = sp[k] - sp[k - 1]
                tm[k - 1] = sm[k] - sm[k - 1]
            i = k - 1
            if first <= i <= last:
                fix[i] = correction(wp[i - 1][0], wp[i][1], wp[i + 1][2], tp[i - 1], tp[i])
            i, c = k - 2, k - 1
            if first <= i <= last:
                fix_m = correction(wm[c + 1][2], wm[c][1], wm[c - 1][0], tm[c], tm[c - 1])
                emit(i, face_value(gp[i], gm[c], dp[i - 1], dp[i], dm[i], dm[c], fix[i], fix_m))


def ring_differences(gp, gm):
    n = len(gp)

    def up(x):
        return [x[(i + 1) % n] for i in range(n)]

    def down(x):
        return [x[(i - 1) % n] for i in range(n)]

    def parts(g):
        d = [b - a for a, b in zip(g, up(g))]
        q = [a * a for a in d]
        terms = [cell_terms(*each) for each in zip(down(d), d, down(q), q)]
        s, low, mid, high = map(list, zip(*terms))
        t = [b - a for a, b in zip(s, up(s))]
        return d, t, low, mid, high

    dp, t, low, mid, high = parts(gp)
    fix_p = [correction(*each) for each in zip(down(low), mid, up(high), down(t), t)]
    dm, t, low, mid, high = parts(gm)
    fix_m = [correction(*each) for each in zip(up(high), mid, down(low), t, down(t))]
    faces = [
        face_value(*each) for each in zip(gp, up(gm), down(dp), dp, dm, up(dm), fix_p, up(fix_m))
    ]
    return [a - b for a, b in zip(faces, down(faces))]


def one_side(far, near, centre, ahead, beyond):
    d1, d2, d3, d4 = near - far, centre - near, ahead - centre, beyond - ahead
    q2, q3 = d2 * d2, d3 * d3
    r_far = reciprocal(d1 * (d1 - 2.75 * d2) + (2.5 * q2 + 1.5 * EPS))
    r_mid = reciprocal(d2 * (d2 - 1.25 * d3) + (q3 + 1.5 * EPS))
    r_near = reciprocal(d4 * (d4 - 2.75 * d3) + (2.5 * q3 + 1.5 * EPS))
    s0, s1, s2 = d2 - d1, d3 - d2, d4 - d3
    fix = correction(r_far * r_far, 6.0 * (r_mid * r_mid), r_near * r_near, s1 - s0, s2 - s1)
    return d2, d3, fix


def shifted_copies(gp, gm):
    return [roll(gp, k) for k in (2, 1, 0, -1, -2)] + [roll(gm, k) for k in (-3, -2, -1, 0, 1)]


def lane_faces(copies):
    low, high, fix_p = one_side(*copies[:5])
    back, front, fix_m = one_side(*copies[5:])
    inner = (high + front) - (fix_p + fix_m)
    return 6.0 * (copies[2] + copies[7]) + (low + back) + 2.0 * inner


def primitives(rho, m1, m2, m3, energy, reactant):
    inverse = reciprocal(rho)
    v1, v2, v3 = m1 * inverse, m2 * inverse, m3 * inverse
    kinetic = 0.5 * (m1 * v1 + m2 * v2 + m3 * v3)
    return v1, v2, v3, 0.4 * (energy - kinetic - reactant)


def signal_speed(rho, m1, m2, m3, energy, reactant):
    press = primitives(rho, m1, m2, m3, energy, reactant)[3]
    inverse = reciprocal(rho)
    fastest = jnp.maximum(jnp.maximum(jnp.abs(m1), jnp.abs(m2)), jnp.abs(m3))
    return fastest * inverse + jnp.sqrt(1.4 * press * inverse)


def kernel(
    nx, ny, state, inflow, out,
    raw, infl, turned, fields, prim, halo_prim, lined, acc, faces,
    windows, edges, ninth_p, ninth_m, ninth_d, pack, from_left, from_right, halo, peak_x, peak_y, consts,
    local_sem, send_sem, recv_sem,
):
    me_x, me_y = lax.axis_index("gx"), lax.axis_index("gy")
    is_first, is_last = me_x == 0, me_x == nx - 1
    lane = lax.broadcasted_iota(jnp.int32, (8, LANES), 1)
    sub = lax.broadcasted_iota(jnp.int32, (8, LANES), 0)
    place = lane & 15

    def peer(dx, dy):
        return (lax.rem(me_x + (dx + nx), nx), lax.rem(me_y + (dy + ny), ny))

    def remote(src, dst, slot, target):
        return pltpu.make_async_remote_copy(
            src_ref=src, dst_ref=dst, send_sem=send_sem.at[slot], recv_sem=recv_sem.at[slot],
            device_id=target, device_id_type=MESH,
        )

    fetch_state = pltpu.make_async_copy(state, raw, local_sem.at[0])
    fetch_inflow = pltpu.make_async_copy(inflow, infl, local_sem.at[1])
    fetch_state.start()
    fetch_inflow.start()
    barrier = pltpu.get_barrier_semaphore()
    for k in range(1, nx):
        pl.semaphore_signal(barrier, inc=1, device_id=peer(k, 0), device_id_type=MESH)
    for k in range(1, ny):
        pl.semaphore_signal(barrier, inc=1, device_id=peer(0, k), device_id_type=MESH)
    fetch_state.wait()
    fetch_inflow.wait()

    def tile_speed(ref, tile, stride):
        rows = [ref[pl.ds(stride * c + 8 * tile, 8), :] for c in range(6)]
        return signal_speed(*rows)

    peak = tile_speed(raw, 0, 64)
    for g in range(1, GROUPS):
        peak = jnp.maximum(peak, tile_speed(raw, g, 64))
    entering = tile_speed(infl, 0, 32)
    for z in range(1, NZ):
        entering = jnp.maximum(entering, tile_speed(infl, z, 32))
    peak = jnp.where(is_first & (lane < 8), 0.0, peak)
    peak_x[pl.ds(0, 8), :] = jnp.maximum(peak, jnp.max(entering))

    def opening_block(g, q):
        if q == 8:
            return raw[pl.ds(64 * 8 + 8 * g, 8), :]
        return raw[pl.ds(8 * g + q, 8, stride=64), :]

    for q in range(BLOCKS):
        head = jnp.zeros((8, LANES), jnp.float32)
        own = head
        for g in range(GROUPS):
            block = opening_block(g, q)
            here = (lane >> 4) == g
            head = jnp.where(here, roll(block, 16 * g + 5), head)
            own = jnp.where(here, roll(block, 16 * g - 5), own)
        pack[0, pl.ds(8 * q, 8), :] = head
        windows[pl.ds(8 * q, 8), :] = own

    pl.semaphore_wait(barrier, nx + ny - 2)

    def spread(buffer, count, base, step):
        copies = []
        for k in range(1, count):
            copies.append(
                remote(buffer.at[pl.ds(0, 8)], buffer.at[pl.ds(8 * k, 8)], base + k, peer(*step(k)))
            )
            copies[-1].start()
        return copies

    def gather(buffer, copies):
        total = buffer[pl.ds(0, 8), :]
        for k, copy in enumerate(copies):
            copy.wait_recv()
            total = jnp.maximum(total, buffer[pl.ds(8 * (k + 1), 8), :])
        return total

    sent_x = spread(peak_x, nx, 0, lambda k: (k, 0))

    shift_copy = remote(pack.at[0], from_right.at[0], 2 * 16, peer(-1, 0))

    @pl.when(me_x > 0)
    def _():
        shift_copy.start()

    @pl.when(is_last)
    def _():
        for c in range(COMPS):
            turned[pl.ds(16 * c, 16), 0:32] = infl[pl.ds(32 * c, 32), :].T
        for q in range(BLOCKS):
            head = jnp.zeros((8, LANES), jnp.float32)
            for g in range(GROUPS):
                z, t = g // 2, g % 2
                rows = pl.ds(8 * t + q, 8, stride=16) if q < 8 else pl.ds(128 + 8 * t, 8)
                block = roll(turned[rows, :], 16 * g + 5 - 8 * z)
                head = jnp.where((lane >> 4) == g, block, head)
            for k in range(1, 4):
                head = jnp.where(place == 12 + k, roll(head, k), head)
            from_right[0, pl.ds(8 * q, 8), :] = head

    peak_y[pl.ds(0, 8), :] = gather(peak_x, sent_x)
    sent_y = spread(peak_y, ny, 16, lambda k: (0, k))

    @pl.when(jnp.logical_not(is_last))
    def _():
        shift_copy.wait_recv()

    for q in range(BLOCKS):
        rows = pl.ds(8 * q, 8)
        arrived = from_right[0, rows, :]
        for g in range(GROUPS):
            block = opening_block(g, q)
            block = jnp.where(lane < LANES - 8, roll(block, -8), roll(arrived, 115 - 16 * g))
            fields[0, g // 2, g % 2, rows, :] = block
        own = windows[rows, :]
        edge = own
        for k in range(1, 4):
            edge = jnp.where(place == 3 - k, roll(own, -k), edge)
        own = jnp.where(is_first, edge, own)
        windows[rows, :] = jnp.where(place < 8, own, arrived)

    def y_copies(stage):
        now, base = fields.at[stage], 33 + 3 * stage
        low, high = halo.at[stage, 0], halo.at[stage, 1]
        return [
            remote(now.at[:, 1, 40:72, :], low, base, peer(0, 1)),
            remote(now.at[:, 0, 0:24, :], high.at[:, 0:24, :], base + 1, peer(0, -1)),
            remote(now.at[:, 0, 64:72, :], high.at[:, 24:32, :], base + 2, peer(0, -1)),
        ]

    def x_copies(stage):
        base = 42 + 2 * (stage - 1)
        return [
            remote(pack.at[stage], from_left.at[stage], base, peer(1, 0)),
            remote(pack.at[stage], from_right.at[stage], base + 1, peer(-1, 0)),
        ]

    for copy in y_copies(0):
        copy.start()

    top = jnp.max(gather(peak_y, sent_y))
    speed = jnp.full((8, LANES), top, jnp.float32)
    consts[0] = speed
    consts[1] = COURANT / speed

    def fluxes(block, velocity, press, lam, component):
        flow = velocity * (block + jnp.where(sub == 4, press, 0.0))
        flow = flow + jnp.where(sub == component, press, 0.0)
        move = lam * block
        return flow + move, flow - move

    def ninth_fluxes(block, velocity, lam):
        flow, move = velocity * block, lam * block
        return flow + move, flow - move

    for stage in range(3):
        now = fields.at[stage]
        lam = consts[0]

        for g in range(GROUPS):
            rows = [now[g // 2, g % 2, pl.ds(c, 8, stride=8), :] for c in range(6)]
            for index, value in enumerate(primitives(*rows)):
                prim[index, g] = value

        def spanwise(t, _):
            for q in range(BLOCKS):
                rows = pl.ds(8 * q, 8)
                gp, gm = [], []
                for z in range(NZ):
                    block = now[z, t, rows, :]
                    if q < 8:
                        v1, v3, press = (prim[i, 2 * z + t, q : q + 1, :] for i in (0, 2, 3))
                        one = fluxes(block, v1, press, lam, 1)
                        three = fluxes(block, v3, press, lam, 3)
                    else:
                        one = ninth_fluxes(block, prim[0, 2 * z + t], lam)
                        three = ninth_fluxes(block, prim[2, 2 * z + t], lam)
                    for k, value in enumerate(shifted_copies(*one)):
                        lined[k, z, t, rows, :] = value
                    gp.append(three[0])
                    gm.append(three[1])
                for z, value in enumerate(ring_differences(gp, gm)):
                    acc[z, t, rows, :] = value
            return 0

        lax.fori_loop(0, 2, spanwise, 0)

        def streamwise(g, _):
            z, t = g // 2, g % 2
            for q in range(BLOCKS):
                rows = pl.ds(8 * q, 8)
                faces[z, t, rows, :] = lane_faces([lined[k, z, t, rows, :] for k in range(10)])
            return 0

        lax.fori_loop(0, GROUPS, streamwise, 0)

        if stage > 0:
            left, right = x_copies(stage)

            @pl.when(me_x > 0)
            def _():
                left.wait_recv()

            @pl.when(jnp.logical_not(is_last))
            def _():
                right.wait_recv()

            for q in range(BLOCKS):
                rows = pl.ds(8 * q, 8)
                own = pack[stage, rows, :]
                low, high = own, own
                for k in range(1, 4):
                    low = jnp.where(place == 3 - k, roll(own, -k), low)
                    high = jnp.where(place == 12 + k, roll(own, k), high)
                low = jnp.where(is_first, low, from_left[stage, rows, :])
                high = jnp.where(is_last, high, from_right[stage, rows, :])
                windows[rows, :] = jnp.where(place < 3, low, jnp.where(place > 12, high, own))

        rows6 = [windows[pl.ds(c, 8, stride=8), :] for c in range(6)]
        v1, _, _, press = primitives(*rows6)
        edges[0, pl.ds(0, 8), :] = v1
        edges[0, pl.ds(8, 8), :] = press
        for q in range(BLOCKS):
            rows = pl.ds(8 * q, 8)
            block = windows[rows, :]
            if q < 8:
                pair = fluxes(block, edges[0, q : q + 1, :], edges[0, 8 + q : 9 + q, :], lam, 1)
            else:
                pair = ninth_fluxes(block, v1, lam)
            face = lane_faces(shifted_copies(*pair))
            edges[1, rows, :] = jnp.where(place < 3, roll(face, -9), roll(face, 1))
            edges[2, rows, :] = jnp.where(place < 3, roll(face, -10), face)

        for copy in y_copies(stage):
            copy.wait_recv()
        for side in range(2):
            for z in range(NZ):
                rows = [halo[stage, side, z, pl.ds(c, 3, stride=8), :] for c in range(6)]
                _, v2, _, press = primitives(*rows)
                start = 5 if side == 0 else 0
                halo_prim[0, side, z, start : start + 3, :] = v2
                halo_prim[1, side, z, start : start + 3, :] = press

        def streamwise_difference(z, t, q):
            rows = pl.ds(8 * q, 8)
            back = 125 - 32 * z - 16 * t
            face = faces[z, t, rows, :]
            under = jnp.where(
                (lane < 3) | (lane > 125), pltpu.roll(edges[1, rows, :], back, axis=1), roll(face, 1)
            )
            face = jnp.where(
                (lane < 2) | (lane > 124), pltpu.roll(edges[2, rows, :], back, axis=1), face
            )
            return face - under

        def transverse(z, _):
            def load(j):
                if 0 <= j < NY:
                    t, q = j // 8, j % 8
                    block = now[z, t, pl.ds(8 * q, 8), :]
                    v2, press = (prim[i, 2 * z + t, q : q + 1, :] for i in (1, 3))
                else:
                    side, q = (0, j + 8) if j < 0 else (1, j - NY)
                    block = halo[stage, side, z, pl.ds(8 * (j + 3 if j < 0 else q), 8), :]
                    v2, press = (halo_prim[i, side, z, q : q + 1, :] for i in (0, 1))
                return fluxes(block, v2, press, lam, 2)

            before = {}

            def emit(i, face):
                before[i] = face
                if i >= 0:
                    t, q = i // 8, i % 8
                    total = (face - before.pop(i - 1)) + streamwise_difference(z, t, q)
                    acc[z, t, pl.ds(8 * q, 8), :] += total

            stream_faces(load, -1, NY - 1, emit)
            for t in range(2):
                acc[z, t, pl.ds(64, 8), :] += streamwise_difference(z, t, 8)

            tiles = [
                (halo[stage, 0, z, pl.ds(24, 8), :], halo_prim[0, 0, z]),
                (now[z, 0, pl.ds(64, 8), :], prim[1, 2 * z]),
                (now[z, 1, pl.ds(64, 8), :], prim[1, 2 * z + 1]),
                (halo[stage, 1, z, pl.ds(24, 8), :], halo_prim[0, 1, z]),
            ]
            for index, (block, v2) in enumerate(tiles):
                plus, minus = ninth_fluxes(block, v2, lam)
                for h in range(2):
                    if 0 <= index - h < 3:
                        start = pl.multiple_of(24 * z + 96 * h + 8 * (index - h), 8)
                        ninth_p[pl.ds(start, 8), :] = plus
                        ninth_m[pl.ds(start, 8), :] = minus
            return 0

        lax.fori_loop(0, NZ, transverse, 0)

        before = {}

        def emit_ninth(i, face):
            before[i] = face
            if i >= 0:
                ninth_d[pl.ds(i, 8, stride=8), :] = face - before.pop(i - 1)

        def load_ninth(j):
            rows = pl.ds(8 + j, 8, stride=24)
            return ninth_p[rows, :], ninth_m[rows, :]

        stream_faces(load_ninth, -1, 7, emit_ninth)
        for h in range(2):
            for z in range(NZ):
                acc[z, h, pl.ds(64, 8), :] += ninth_d[pl.ds(8 * (4 * h + z), 8), :]

        keep, blend = STAGES[stage]

        scale = consts[1] * (blend / 12.0)
        for q in range(BLOCKS):
            rows = pl.ds(8 * q, 8)
            packed = jnp.zeros((8, LANES), jnp.float32)
            for g in range(GROUPS):
                z, t = g // 2, g % 2
                value = now[z, t, rows, :]
                if stage > 0:
                    value = keep * fields[0, z, t, rows, :] + blend * value
                value = value - scale * acc[z, t, rows, :]
                fields[stage + 1, z, t, rows, :] = value
                if stage < 2:
                    here = (lane >> 4) == g
                    ends = jnp.where(place < 8, roll(value, 16 * g + 3), roll(value, 16 * g + 13))
                    packed = jnp.where(here, ends, packed)
            if stage < 2:
                pack[stage + 1, rows, :] = packed

        if stage < 2:
            for copy in y_copies(stage + 1):
                copy.start()
            left, right = x_copies(stage + 1)

            @pl.when(jnp.logical_not(is_last))
            def _():
                left.start()

            @pl.when(me_x > 0)
            def _():
                right.start()

    third = fields.at[3]

    for g in range(GROUPS):
        z, t = g // 2, g % 2
        rows = [third[z, t, pl.ds(c, 8, stride=8), :] for c in range(8)]
        rho, m1, m2, m3, energy, reactant, product, other = rows
        inverse = reciprocal(rho)
        rest = energy - 0.5 * (m1 * m1 + m2 * m2 + m3 * m3) * inverse
        small = consts[1] * (PREFACTOR / SUBSTEPS)
        for _ in range(SUBSTEPS):
            press = 0.4 * (rest - reactant)
            burned = small * reactant * jnp.exp(-ACTIVATION * (rho * reciprocal(press)))
            reactant, product = reactant - burned, product + burned
        rows = [rho, m1, m2, m3, energy, reactant, product, other, third[z, t, pl.ds(64, 8), :]]
        for c, value in enumerate(rows):
            out[pl.ds(64 * c + 8 * g, 8), :] = value

    for copy in sent_x + sent_y + y_copies(0) + y_copies(1) + y_copies(2):
        copy.wait_send()
    for stage in (1, 2):
        left, right = x_copies(stage)

        @pl.when(jnp.logical_not(is_last))
        def _():
            left.wait_send()

        @pl.when(me_x > 0)
        def _():
            right.wait_send()

    @pl.when(me_x > 0)
    def _():
        shift_copy.wait_send()


def on_device(nx, ny, state, inflow):
    rows = COMPS * NZ * NY
    f32 = jnp.float32

    inflow = jnp.swapaxes(inflow, 2, 3).reshape(COMPS * NZ * inflow.shape[3], NY)

    def vmem(*shape):
        return pltpu.VMEM(shape, f32)

    result = pl.pallas_call(
        functools.partial(kernel, nx, ny),
        out_shape=jax.ShapeDtypeStruct((rows, LANES), f32),
        in_specs=[pl.BlockSpec(memory_space=pltpu.HBM)] * 2,
        out_specs=pl.BlockSpec(memory_space=pltpu.VMEM),
        scratch_shapes=[
            vmem(rows, LANES),
            vmem(*inflow.shape),
            vmem(COMPS * NY, LANES),
            vmem(4, NZ, 2, 72, LANES),
            vmem(4, GROUPS, 8, LANES),
            vmem(2, 2, NZ, 8, LANES),
            vmem(10, NZ, 2, 72, LANES),
            vmem(NZ, 2, 72, LANES),
            vmem(NZ, 2, 72, LANES),
            vmem(72, LANES),
            vmem(3, 72, LANES),
            vmem(192, LANES),
            vmem(192, LANES),
            vmem(64, LANES),
            vmem(3, 72, LANES),
            vmem(3, 72, LANES),
            vmem(3, 72, LANES),
            vmem(3, 2, NZ, 32, LANES),
            vmem(8 * 16, LANES),
            vmem(8 * 16, LANES),
            vmem(2, 8, LANES),
            pltpu.SemaphoreType.DMA((2,)),
            pltpu.SemaphoreType.DMA((46,)),
            pltpu.SemaphoreType.DMA((46,)),
        ],
        compiler_params=pltpu.CompilerParams(
            collective_id=0, has_side_effects=True, vmem_limit_bytes=60 * 1024 * 1024
        ),
        cost_estimate=pl.CostEstimate(
            flops=60_000_000, bytes_accessed=1_200_000, transcendentals=5_000_000
        ),
    )(state.reshape(rows, LANES), inflow)
    return result.reshape(state.shape)


def solution(mesh):
    return jax.shard_map(
        functools.partial(on_device, mesh.shape["gx"], mesh.shape["gy"]),
        mesh=mesh,
        in_specs=(P(None, None, "gy", "gx"), P(None, None, "gy", None)),
        out_specs=P(None, None, "gy", "gx"),
        check_vma=False,
    )
```

```python
import functools

import jax
import jax.numpy as jnp
from jax import lax
from jax.experimental import pallas as pl
from jax.experimental.pallas import tpu as pltpu
from jax.sharding import PartitionSpec as P

MESH = pl.DeviceIdType.MESH
NZ = 4
NY = 16
LANES = 128
COMPS = 9
GROUPS = 8
BLOCKS = 9
SUBSTEPS = 4
PREFACTOR = 300.0
ACTIVATION = 4.0
COURANT = 0.15
EPS = 2e-6
STAGES = ((0.0, 1.0), (0.75, 0.25), (1.0 / 3.0, 2.0 / 3.0))


def reciprocal(x):
    return pltpu.reciprocal(x, approx=True)


def roll(x, shift):
    shift = shift % LANES
    return x if shift == 0 else pltpu.roll(x, shift, axis=1)


def cell_terms(d_low, d_high, q_low, q_high):
    second = d_high - d_low
    half = d_low * (0.5 * d_high)
    level = (2.0 / 3.0) * (second * second) + EPS
    base = level - half
    r_low = reciprocal(base + q_high)
    r_mid = reciprocal(level + half)
    r_high = reciprocal(base + q_low)
    return second, r_low * r_low, 6.0 * (r_mid * r_mid), r_high * r_high


def correction(w_far, w_mid, w_near, t_far, t_near):
    near = 3.0 * w_near
    return (w_far * t_far + near * (0.5 * t_near)) * reciprocal((w_far + w_mid) + near)


def face_value(gp, gm, dp_low, dp_high, dm_low, dm_high, fix_p, fix_m):
    inner = (dp_high - dm_low) - (fix_p - fix_m)
    return 6.0 * (gp + gm) + (dp_low - dm_high) + 2.0 * inner


def stream_faces(load, first, last, emit):
    gp, gm, dp, dm, qp, qm = {}, {}, {}, {}, {}, {}
    tp, tm, sp, sm, wp, wm = {}, {}, {}, {}, {}, {}
    fix = {}
    for j in range(first - 2, last + 4):
        gp[j], gm[j] = load(j)
        k = j - 1
        if j > first - 2:
            dp[k] = gp[j] - gp[k]
            qp[k] = dp[k] * dp[k]
            dm[k] = gm[j] - gm[k]
            qm[k] = dm[k] * dm[k]
        if j >= first:
            sp[k], *wp[k] = cell_terms(dp[k - 1], dp[k], qp[k - 1], qp[k])
            sm[k], *wm[k] = cell_terms(dm[k - 1], dm[k], qm[k - 1], qm[k])
            if k > first - 1:
                tp[k - 1] = sp[k] - sp[k - 1]
                tm[k - 1] = sm[k] - sm[k - 1]
            i = k - 1
            if first <= i <= last:
                fix[i] = correction(wp[i - 1][0], wp[i][1], wp[i + 1][2], tp[i - 1], tp[i])
            i, c = k - 2, k - 1
            if first <= i <= last:
                fix_m = correction(wm[c + 1][2], wm[c][1], wm[c - 1][0], tm[c], tm[c - 1])
                emit(i, face_value(gp[i], gm[c], dp[i - 1], dp[i], dm[i], dm[c], fix[i], fix_m))


def ring_differences(gp, gm):
    n = len(gp)

    def up(x):
        return [x[(i + 1) % n] for i in range(n)]

    def down(x):
        return [x[(i - 1) % n] for i in range(n)]

    def parts(g):
        d = [b - a for a, b in zip(g, up(g))]
        q = [a * a for a in d]
        terms = [cell_terms(*each) for each in zip(down(d), d, down(q), q)]
        s, low, mid, high = map(list, zip(*terms))
        t = [b - a for a, b in zip(s, up(s))]
        return d, t, low, mid, high

    dp, t, low, mid, high = parts(gp)
    fix_p = [correction(*each) for each in zip(down(low), mid, up(high), down(t), t)]
    dm, t, low, mid, high = parts(gm)
    fix_m = [correction(*each) for each in zip(up(high), mid, down(low), t, down(t))]
    faces = [
        face_value(*each) for each in zip(gp, up(gm), down(dp), dp, dm, up(dm), fix_p, up(fix_m))
    ]
    return [a - b for a, b in zip(faces, down(faces))]


def one_side(far, near, centre, ahead, beyond):
    d1, d2, d3, d4 = near - far, centre - near, ahead - centre, beyond - ahead
    q2, q3 = d2 * d2, d3 * d3
    r_far = reciprocal(d1 * (d1 - 2.75 * d2) + (2.5 * q2 + 1.5 * EPS))
    r_mid = reciprocal(d2 * (d2 - 1.25 * d3) + (q3 + 1.5 * EPS))
    r_near = reciprocal(d4 * (d4 - 2.75 * d3) + (2.5 * q3 + 1.5 * EPS))
    s0, s1, s2 = d2 - d1, d3 - d2, d4 - d3
    fix = correction(r_far * r_far, 6.0 * (r_mid * r_mid), r_near * r_near, s1 - s0, s2 - s1)
    return d2, d3, fix


def shifted_copies(gp, gm):
    return [roll(gp, k) for k in (2, 1, 0, -1, -2)] + [roll(gm, k) for k in (-3, -2, -1, 0, 1)]


def lane_faces(copies):
    low, high, fix_p = one_side(*copies[:5])
    back, front, fix_m = one_side(*copies[5:])
    inner = (high + front) - (fix_p + fix_m)
    return 6.0 * (copies[2] + copies[7]) + (low + back) + 2.0 * inner


def exchange_groups(nx, ny):
    cores = 2 - nx % 2
    width = min(4, nx // cores)
    depth = nx // (cores * width)
    low = 2 - ny % 2
    length = ny // low
    plane, column = [], []
    for a in range(depth):
        for b in range(width):
            for c in range(low):
                far = min(b, width - b) + (2 if a else c)
                plane.append((far, (a, b, 0, 0, c)))
    for d in range(length):
        for e in range(cores):
            column.append((min(d, length - d) + 0.2 * e, (0, 0, e, d, 0)))
    sizes = (depth, width, cores, length, low)
    plane, column = (
        [x for x in sorted(group, key=lambda x: -x[0]) if any(x[1])] for group in (plane, column)
    )
    return sizes, plane, column


def primitives(rho, m1, m2, m3, energy, reactant):
    inverse = reciprocal(rho)
    v1, v2, v3 = m1 * inverse, m2 * inverse, m3 * inverse
    kinetic = 0.5 * (m1 * v1 + m2 * v2 + m3 * v3)
    return v1, v2, v3, 0.4 * (energy - kinetic - reactant)


def signal_speed(rho, m1, m2, m3, energy, reactant):
    press = primitives(rho, m1, m2, m3, energy, reactant)[3]
    inverse = reciprocal(rho)
    fastest = jnp.maximum(jnp.maximum(jnp.abs(m1), jnp.abs(m2)), jnp.abs(m3))
    return fastest * inverse + jnp.sqrt(1.4 * press * inverse)


def kernel(
    nx, ny, state, inflow, out,
    raw, infl, turned, fields, prim, halo_prim, lined, acc, faces,
    windows, edges, ninth_p, ninth_m, ninth_d, ninth_out, ninth_in, ninth_halo, pack, opening,
    ends_out, ends_in, halo, peaks, consts,
    local_sem, send_sem, recv_sem,
):
    me_x, me_y = lax.axis_index("gx"), lax.axis_index("gy")
    is_first, is_last = me_x == 0, me_x == nx - 1
    lane = lax.broadcasted_iota(jnp.int32, (8, LANES), 1)
    sub = lax.broadcasted_iota(jnp.int32, (8, LANES), 0)
    place = lane & 15

    sizes, plane, column = exchange_groups(nx, ny)
    _, n_x, n_core, _, n_low = sizes
    digits = (
        me_x // (n_x * n_core), (me_x // n_core) % n_x, me_x % n_core, me_y // n_low, me_y % n_low
    )

    def peer(dx, dy):
        return (lax.rem(me_x + (dx + nx), nx), lax.rem(me_y + (dy + ny), ny))

    def partner(offset):
        a, b, c, d, e = (
            x if o == 0 else lax.rem(x + o, n) for x, o, n in zip(digits, offset, sizes)
        )
        return ((a * n_x + b) * n_core + c, d * n_low + e)

    def remote(src, dst, slot, target):
        return pltpu.make_async_remote_copy(
            src_ref=src, dst_ref=dst, send_sem=send_sem.at[slot], recv_sem=recv_sem.at[slot],
            device_id=target, device_id_type=MESH,
        )

    fetch_state = pltpu.make_async_copy(state, raw, local_sem.at[0])
    fetch_inflow = pltpu.make_async_copy(inflow, infl, local_sem.at[1])
    fetch_state.start()
    fetch_inflow.start()
    barrier = pltpu.get_barrier_semaphore()
    greeted = [partner(offset) for _, offset in sorted(plane + column, key=lambda x: -x[0])]
    greeted += [peer(1, 0), peer(-1, 0), peer(0, 1), peer(0, -1)]
    for device in greeted:
        pl.semaphore_signal(barrier, inc=1, device_id=device, device_id_type=MESH)
    fetch_state.wait()
    fetch_inflow.wait()

    def tile_speed(ref, tile, stride):
        rows = [ref[pl.ds(stride * c + 8 * tile, 8), :] for c in range(6)]
        return signal_speed(*rows)

    peak = tile_speed(raw, 0, 64)
    for g in range(1, GROUPS):
        peak = jnp.maximum(peak, tile_speed(raw, g, 64))
    entering = tile_speed(infl, 0, 32)
    for z in range(1, NZ):
        entering = jnp.maximum(entering, tile_speed(infl, z, 32))
    peak = jnp.where(is_first & (lane < 8), 0.0, peak)
    top = jnp.maximum(jnp.max(peak), jnp.max(entering))
    peaks[0, 0:1, :] = jnp.full((1, LANES), top, jnp.float32)

    pl.semaphore_wait(barrier, len(greeted))

    def phase_copy(phase, rows, device):
        return remote(
            peaks.at[phase, pl.ds(0, rows)], peaks.at[phase, pl.ds(1, rows)], phase, device
        )

    def send_peak(phase, group):
        for k, (_, offset) in enumerate(group):
            remote(
                peaks.at[phase, pl.ds(0, 1)], peaks.at[phase, pl.ds(k + 1, 1)], phase, partner(offset)
            ).start()

    def largest(phase, group):
        phase_copy(phase, len(group), partner(group[0][1])).wait_recv()
        return jnp.max(peaks[phase, pl.ds(0, len(group) + 1), :], axis=0, keepdims=True)

    send_peak(0, plane)

    def opening_block(g, q):
        if q == 8:
            return raw[pl.ds(64 * 8 + 8 * g, 8), :]
        return raw[pl.ds(8 * g + q, 8, stride=64), :]

    for q in range(BLOCKS):
        head = jnp.zeros((8, LANES), jnp.float32)
        own = head
        for g in range(GROUPS):
            block = opening_block(g, q)
            here = (lane >> 4) == g
            head = jnp.where(here, roll(block, 16 * g + 5), head)
            own = jnp.where(here, roll(block, 16 * g - 5), own)
        pack[0, pl.ds(8 * q, 8), :] = head
        windows[pl.ds(8 * q, 8), :] = own

    shift_copy = remote(pack.at[0, pl.ds(0, 72)], opening, 2, peer(-1, 0))

    @pl.when(me_x > 0)
    def _():
        shift_copy.start()

    @pl.when(is_last)
    def _():
        for c in range(COMPS):
            turned[pl.ds(16 * c, 16), 0:32] = infl[pl.ds(32 * c, 32), :].T
        for q in range(BLOCKS):
            head = jnp.zeros((8, LANES), jnp.float32)
            for g in range(GROUPS):
                z, t = g // 2, g % 2
                rows = pl.ds(8 * t + q, 8, stride=16) if q < 8 else pl.ds(128 + 8 * t, 8)
                block = roll(turned[rows, :], 16 * g + 5 - 8 * z)
                head = jnp.where((lane >> 4) == g, block, head)
            for k in range(1, 4):
                head = jnp.where(place == 12 + k, roll(head, k), head)
            opening[pl.ds(8 * q, 8), :] = head

    peaks[1, 0:1, :] = largest(0, plane)
    send_peak(1, column)

    @pl.when(jnp.logical_not(is_last))
    def _():
        shift_copy.wait_recv()

    for q in range(BLOCKS):
        rows = pl.ds(8 * q, 8)
        arrived = opening[rows, :]
        for g in range(GROUPS):
            block = opening_block(g, q)
            block = jnp.where(lane < LANES - 8, roll(block, -8), roll(arrived, 115 - 16 * g))
            fields[0, g // 2, g % 2, rows, :] = block
        own = windows[rows, :]
        edge = own
        for k in range(1, 4):
            edge = jnp.where(place == 3 - k, roll(own, -k), edge)
        own = jnp.where(is_first, edge, own)
        windows[rows, :] = jnp.where(place < 8, own, arrived)

    def pack_ninth(stage):
        for z in range(NZ):
            ninth_out[stage, 0, 4 * z : 4 * z + 3, :] = fields[stage, z, 1, 69:72, :]
            ninth_out[stage, 1, 4 * z : 4 * z + 3, :] = fields[stage, z, 0, 64:67, :]

    def y_copies(stage):
        now, base = fields.at[stage], 3 + 4 * stage
        up, down = peer(0, 1), peer(0, -1)
        return [
            remote(now.at[:, 1, 40:64, :], halo.at[stage, 0], base, up),
            remote(now.at[:, 0, 0:24, :], halo.at[stage, 1], base + 1, down),
            remote(ninth_out.at[stage, 0], ninth_in.at[stage, 0], base + 2, up),
            remote(ninth_out.at[stage, 1], ninth_in.at[stage, 1], base + 3, down),
        ]

    def x_copies(stage):
        base = 15 + 2 * (stage - 1)
        return [
            remote(ends_out.at[stage - 1, 0], ends_in.at[stage - 1, 0], base, peer(1, 0)),
            remote(ends_out.at[stage - 1, 1], ends_in.at[stage - 1, 1], base + 1, peer(-1, 0)),
        ]

    pack_ninth(0)
    for copy in y_copies(0):
        copy.start()

    def fluxes(block, velocity, press, lam, component):
        flow = velocity * (block + jnp.where(sub == 4, press, 0.0))
        flow = flow + jnp.where(sub == component, press, 0.0)
        move = lam * block
        return flow + move, flow - move

    def ninth_fluxes(block, velocity, lam):
        flow, move = velocity * block, lam * block
        return flow + move, flow - move

    for stage in range(3):
        now = fields.at[stage]
        for g in range(GROUPS):
            rows = [now[g // 2, g % 2, pl.ds(c, 8, stride=8), :] for c in range(6)]
            for index, value in enumerate(primitives(*rows)):
                prim[index, g] = value

        if stage == 0:
            speed = jnp.broadcast_to(largest(1, column), (8, LANES))
            consts[0] = speed
            consts[1] = COURANT / speed
        lam = consts[0]

        def spanwise(t, _):
            for q in range(BLOCKS):
                rows = pl.ds(8 * q, 8)
                gp, gm = [], []
                for z in range(NZ):
                    block = now[z, t, rows, :]
                    if q < 8:
                        v1, v3, press = (prim[i, 2 * z + t, q : q + 1, :] for i in (0, 2, 3))
                        one = fluxes(block, v1, press, lam, 1)
                        three = fluxes(block, v3, press, lam, 3)
                    else:
                        one = ninth_fluxes(block, prim[0, 2 * z + t], lam)
                        three = ninth_fluxes(block, prim[2, 2 * z + t], lam)
                    for k, value in enumerate(shifted_copies(*one)):
                        lined[k, z, t, rows, :] = value
                    gp.append(three[0])
                    gm.append(three[1])
                for z, value in enumerate(ring_differences(gp, gm)):
                    acc[z, t, rows, :] = value
            return 0

        lax.fori_loop(0, 2, spanwise, 0)

        def streamwise(g, _):
            z, t = g // 2, g % 2
            for q in range(BLOCKS):
                rows = pl.ds(8 * q, 8)
                faces[z, t, rows, :] = lane_faces([lined[k, z, t, rows, :] for k in range(10)])
            return 0

        lax.fori_loop(0, GROUPS, streamwise, 0)

        if stage > 0:
            left, right = x_copies(stage)

            @pl.when(me_x > 0)
            def _():
                left.wait_recv()

            @pl.when(jnp.logical_not(is_last))
            def _():
                right.wait_recv()

            for q in range(BLOCKS):
                rows = pl.ds(8 * q, 8)
                own = pack[stage, rows, :]
                low, high = own, own
                for k in range(1, 4):
                    low = jnp.where(place == 3 - k, roll(own, -k), low)
                    high = jnp.where(place == 12 + k, roll(own, k), high)
                tile, at = pl.ds(8 * (q // 5), 8), 3 * (q % 5)
                low = jnp.where(is_first, low, roll(ends_in[stage - 1, 0, tile, :], -at))
                high = jnp.where(is_last, high, roll(ends_in[stage - 1, 1, tile, :], 13 - at))
                windows[rows, :] = jnp.where(place < 3, low, jnp.where(place > 12, high, own))

        rows6 = [windows[pl.ds(c, 8, stride=8), :] for c in range(6)]
        v1, _, _, press = primitives(*rows6)
        edges[0, pl.ds(0, 8), :] = v1
        edges[0, pl.ds(8, 8), :] = press
        for q in range(BLOCKS):
            rows = pl.ds(8 * q, 8)
            block = windows[rows, :]
            if q < 8:
                pair = fluxes(block, edges[0, q : q + 1, :], edges[0, 8 + q : 9 + q, :], lam, 1)
            else:
                pair = ninth_fluxes(block, v1, lam)
            face = lane_faces(shifted_copies(*pair))
            edges[1, rows, :] = jnp.where(place < 3, roll(face, -9), roll(face, 1))
            edges[2, rows, :] = jnp.where(place < 3, roll(face, -10), face)

        for copy in y_copies(stage):
            copy.wait_recv()
        for side in range(2):
            for z in range(NZ):
                rows = [halo[stage, side, z, pl.ds(c, 3, stride=8), :] for c in range(6)]
                _, v2, _, press = primitives(*rows)
                start = 5 if side == 0 else 0
                halo_prim[0, side, z, start : start + 3, :] = v2
                halo_prim[1, side, z, start : start + 3, :] = press
                ninth_halo[side, z, start : start + 3, :] = ninth_in[stage, side, 4 * z : 4 * z + 3, :]

        def streamwise_difference(z, t, q):
            rows = pl.ds(8 * q, 8)
            back = 125 - 32 * z - 16 * t
            face = faces[z, t, rows, :]
            under = jnp.where(
                (lane < 3) | (lane > 125), pltpu.roll(edges[1, rows, :], back, axis=1), roll(face, 1)
            )
            face = jnp.where(
                (lane < 2) | (lane > 124), pltpu.roll(edges[2, rows, :], back, axis=1), face
            )
            return face - under

        def transverse(z, _):
            def load(j):
                if 0 <= j < NY:
                    t, q = j // 8, j % 8
                    block = now[z, t, pl.ds(8 * q, 8), :]
                    v2, press = (prim[i, 2 * z + t, q : q + 1, :] for i in (1, 3))
                else:
                    side, q = (0, j + 8) if j < 0 else (1, j - NY)
                    block = halo[stage, side, z, pl.ds(8 * (j + 3 if j < 0 else q), 8), :]
                    v2, press = (halo_prim[i, side, z, q : q + 1, :] for i in (0, 1))
                return fluxes(block, v2, press, lam, 2)

            before = {}

            def emit(i, face):
                before[i] = face
                if i >= 0:
                    t, q = i // 8, i % 8
                    total = (face - before.pop(i - 1)) + streamwise_difference(z, t, q)
                    acc[z, t, pl.ds(8 * q, 8), :] += total

            stream_faces(load, -1, NY - 1, emit)
            for t in range(2):
                acc[z, t, pl.ds(64, 8), :] += streamwise_difference(z, t, 8)

            tiles = [
                (ninth_halo[0, z], halo_prim[0, 0, z]),
                (now[z, 0, pl.ds(64, 8), :], prim[1, 2 * z]),
                (now[z, 1, pl.ds(64, 8), :], prim[1, 2 * z + 1]),
                (ninth_halo[1, z], halo_prim[0, 1, z]),
            ]
            for index, (block, v2) in enumerate(tiles):
                plus, minus = ninth_fluxes(block, v2, lam)
                for h in range(2):
                    if 0 <= index - h < 3:
                        start = pl.multiple_of(24 * z + 96 * h + 8 * (index - h), 8)
                        ninth_p[pl.ds(start, 8), :] = plus
                        ninth_m[pl.ds(start, 8), :] = minus
            return 0

        lax.fori_loop(0, NZ, transverse, 0)

        before = {}

        def emit_ninth(i, face):
            before[i] = face
            if i >= 0:
                ninth_d[pl.ds(i, 8, stride=8), :] = face - before.pop(i - 1)

        def load_ninth(j):
            rows = pl.ds(8 + j, 8, stride=24)
            return ninth_p[rows, :], ninth_m[rows, :]

        stream_faces(load_ninth, -1, 7, emit_ninth)
        for h in range(2):
            for z in range(NZ):
                acc[z, h, pl.ds(64, 8), :] += ninth_d[pl.ds(8 * (4 * h + z), 8), :]

        keep, blend = STAGES[stage]

        scale = consts[1] * (blend / 12.0)

        def update(q, z, t):
            rows = pl.ds(8 * q, 8)
            value = now[z, t, rows, :]
            if stage > 0:
                value = keep * fields[0, z, t, rows, :] + blend * value
            value = value - scale * acc[z, t, rows, :]
            fields[stage + 1, z, t, rows, :] = value
            return value

        outer = [(0, 0), (1, 0), (2, 0), (8, 0), (5, 1), (6, 1), (7, 1), (8, 1)]
        for q, t in outer:
            for z in range(NZ):
                update(q, z, t)
        if stage < 2:
            pack_ninth(stage + 1)
            for copy in y_copies(stage + 1):
                copy.start()

        for q in range(BLOCKS):
            rows = pl.ds(8 * q, 8)
            packed = jnp.zeros((8, LANES), jnp.float32)
            for g in range(GROUPS):
                z, t = g // 2, g % 2
                value = fields[stage + 1, z, t, rows, :] if (q, t) in outer else update(q, z, t)
                if stage < 2:
                    here = (lane >> 4) == g
                    ends = jnp.where(place < 8, roll(value, 16 * g + 3), roll(value, 16 * g + 13))
                    packed = jnp.where(here, ends, packed)
            if stage < 2:
                pack[stage + 1, rows, :] = packed

        def pack_ends(tile, _):
            for side in range(2):
                joined = jnp.zeros((8, LANES), jnp.float32)
                for k in range(5):
                    window = pack[stage + 1, pl.ds(pl.multiple_of(40 * tile + 8 * k, 8), 8), :]
                    moved = roll(window, 3 * k - 13 * side)
                    joined = jnp.where((place >= 3 * k) & (place < 3 * k + 3), moved, joined)
                ends_out[stage, side, pl.ds(pl.multiple_of(8 * tile, 8), 8), :] = joined
            return 0

        if stage < 2:
            lax.fori_loop(0, 2, pack_ends, 0)
            left, right = x_copies(stage + 1)

            @pl.when(jnp.logical_not(is_last))
            def _():
                left.start()

            @pl.when(me_x > 0)
            def _():
                right.start()

    third = fields.at[3]

    for g in range(GROUPS):
        z, t = g // 2, g % 2
        rows = [third[z, t, pl.ds(c, 8, stride=8), :] for c in range(8)]
        rho, m1, m2, m3, energy, reactant, product, other = rows
        inverse = reciprocal(rho)
        rest = energy - 0.5 * (m1 * m1 + m2 * m2 + m3 * m3) * inverse
        small = consts[1] * (PREFACTOR / SUBSTEPS)
        for _ in range(SUBSTEPS):
            press = 0.4 * (rest - reactant)
            burned = small * reactant * jnp.exp(-ACTIVATION * (rho * reciprocal(press)))
            reactant, product = reactant - burned, product + burned
        rows = [rho, m1, m2, m3, energy, reactant, product, other, third[z, t, pl.ds(64, 8), :]]
        for c, value in enumerate(rows):
            out[pl.ds(64 * c + 8 * g, 8), :] = value

    for phase, group in enumerate((plane, column)):
        phase_copy(phase, len(group), partner(group[0][1])).wait_send()
    for copy in y_copies(0) + y_copies(1) + y_copies(2):
        copy.wait_send()
    for stage in (1, 2):
        left, right = x_copies(stage)

        @pl.when(jnp.logical_not(is_last))
        def _():
            left.wait_send()

        @pl.when(me_x > 0)
        def _():
            right.wait_send()

    @pl.when(me_x > 0)
    def _():
        shift_copy.wait_send()


def on_device(nx, ny, state, inflow):
    rows = COMPS * NZ * NY
    f32 = jnp.float32

    inflow = jnp.swapaxes(inflow, 2, 3).reshape(COMPS * NZ * inflow.shape[3], NY)

    def vmem(*shape):
        return pltpu.VMEM(shape, f32)

    result = pl.pallas_call(
        functools.partial(kernel, nx, ny),
        out_shape=jax.ShapeDtypeStruct((rows, LANES), f32),
        in_specs=[pl.BlockSpec(memory_space=pltpu.HBM)] * 2,
        out_specs=pl.BlockSpec(memory_space=pltpu.VMEM),
        scratch_shapes=[
            vmem(rows, LANES),
            vmem(*inflow.shape),
            vmem(COMPS * NY, LANES),
            vmem(4, NZ, 2, 72, LANES),
            vmem(4, GROUPS, 8, LANES),
            vmem(2, 2, NZ, 8, LANES),
            vmem(10, NZ, 2, 72, LANES),
            vmem(NZ, 2, 72, LANES),
            vmem(NZ, 2, 72, LANES),
            vmem(72, LANES),
            vmem(3, 72, LANES),
            vmem(192, LANES),
            vmem(192, LANES),
            vmem(64, LANES),
            vmem(3, 2, 16, LANES),
            vmem(3, 2, 16, LANES),
            vmem(2, NZ, 8, LANES),
            vmem(3, 80, LANES),
            vmem(72, LANES),
            vmem(2, 2, 16, LANES),
            vmem(2, 2, 16, LANES),
            vmem(3, 2, NZ, 24, LANES),
            vmem(2, 32, LANES),
            vmem(2, 8, LANES),
            pltpu.SemaphoreType.DMA((2,)),
            pltpu.SemaphoreType.DMA((20,)),
            pltpu.SemaphoreType.DMA((20,)),
        ],
        compiler_params=pltpu.CompilerParams(
            collective_id=0, has_side_effects=True, vmem_limit_bytes=32 * 1024 * 1024
        ),
        cost_estimate=pl.CostEstimate(
            flops=60_000_000, bytes_accessed=1_200_000, transcendentals=5_000_000
        ),
    )(state.reshape(rows, LANES), inflow)
    return result.reshape(state.shape)


def solution(mesh):
    return jax.shard_map(
        functools.partial(on_device, mesh.shape["gx"], mesh.shape["gy"]),
        mesh=mesh,
        in_specs=(P(None, None, "gy", "gx"), P(None, None, "gy", None)),
        out_specs=P(None, None, "gy", "gx"),
        check_vma=False,
    )
```

```python
import functools

import jax
import jax.numpy as jnp
from jax import lax
from jax.experimental import pallas as pl
from jax.experimental.pallas import tpu as pltpu
from jax.sharding import PartitionSpec as P

MESH = pl.DeviceIdType.MESH
NZ = 4
NY = 16
LANES = 128
COMPS = 9
GROUPS = 8
BLOCKS = 9
SUBSTEPS = 4
PREFACTOR = 300.0
ACTIVATION = 4.0
COURANT = 0.15
EPS = 2e-6
STAGES = ((0.0, 1.0), (0.75, 0.25), (1.0 / 3.0, 2.0 / 3.0))


def reciprocal(x):
    return pltpu.reciprocal(x, approx=True)


def roll(x, shift):
    shift = shift % LANES
    return x if shift == 0 else pltpu.roll(x, shift, axis=1)


def cell_terms(d_low, d_high, q_low, q_high):
    second = d_high - d_low
    half = d_low * (0.5 * d_high)
    level = (2.0 / 3.0) * (second * second) + EPS
    base = level - half
    r_low = reciprocal(base + q_high)
    r_mid = reciprocal(level + half)
    r_high = reciprocal(base + q_low)
    return second, r_low * r_low, 6.0 * (r_mid * r_mid), r_high * r_high


def correction(w_far, w_mid, w_near, t_far, t_near):
    near = 3.0 * w_near
    return (w_far * t_far + near * (0.5 * t_near)) * reciprocal((w_far + w_mid) + near)


def face_value(gp, gm, dp_low, dp_high, dm_low, dm_high, fix_p, fix_m):
    inner = (dp_high - dm_low) - (fix_p - fix_m)
    return 6.0 * (gp + gm) + (dp_low - dm_high) + 2.0 * inner


def stream_faces(load, first, last, emit):
    gp, gm, dp, dm, qp, qm = {}, {}, {}, {}, {}, {}
    tp, tm, sp, sm, wp, wm = {}, {}, {}, {}, {}, {}
    fix = {}
    for j in range(first - 2, last + 4):
        gp[j], gm[j] = load(j)
        k = j - 1
        if j > first - 2:
            dp[k] = gp[j] - gp[k]
            qp[k] = dp[k] * dp[k]
            dm[k] = gm[j] - gm[k]
            qm[k] = dm[k] * dm[k]
        if j >= first:
            sp[k], *wp[k] = cell_terms(dp[k - 1], dp[k], qp[k - 1], qp[k])
            sm[k], *wm[k] = cell_terms(dm[k - 1], dm[k], qm[k - 1], qm[k])
            if k > first - 1:
                tp[k - 1] = sp[k] - sp[k - 1]
                tm[k - 1] = sm[k] - sm[k - 1]
            i = k - 1
            if first <= i <= last:
                fix[i] = correction(wp[i - 1][0], wp[i][1], wp[i + 1][2], tp[i - 1], tp[i])
            i, c = k - 2, k - 1
            if first <= i <= last:
                fix_m = correction(wm[c + 1][2], wm[c][1], wm[c - 1][0], tm[c], tm[c - 1])
                emit(i, face_value(gp[i], gm[c], dp[i - 1], dp[i], dm[i], dm[c], fix[i], fix_m))


def ring_differences(gp, gm):
    n = len(gp)

    def up(x):
        return [x[(i + 1) % n] for i in range(n)]

    def down(x):
        return [x[(i - 1) % n] for i in range(n)]

    def parts(g):
        d = [b - a for a, b in zip(g, up(g))]
        q = [a * a for a in d]
        terms = [cell_terms(*each) for each in zip(down(d), d, down(q), q)]
        s, low, mid, high = map(list, zip(*terms))
        t = [b - a for a, b in zip(s, up(s))]
        return d, t, low, mid, high

    dp, t, low, mid, high = parts(gp)
    fix_p = [correction(*each) for each in zip(down(low), mid, up(high), down(t), t)]
    dm, t, low, mid, high = parts(gm)
    fix_m = [correction(*each) for each in zip(up(high), mid, down(low), t, down(t))]
    faces = [
        face_value(*each) for each in zip(gp, up(gm), down(dp), dp, dm, up(dm), fix_p, up(fix_m))
    ]
    return [a - b for a, b in zip(faces, down(faces))]


def one_side(far, near, centre, ahead, beyond):
    d1, d2, d3, d4 = near - far, centre - near, ahead - centre, beyond - ahead
    q2, q3 = d2 * d2, d3 * d3
    r_far = reciprocal(d1 * (d1 - 2.75 * d2) + (2.5 * q2 + 1.5 * EPS))
    r_mid = reciprocal(d2 * (d2 - 1.25 * d3) + (q3 + 1.5 * EPS))
    r_near = reciprocal(d4 * (d4 - 2.75 * d3) + (2.5 * q3 + 1.5 * EPS))
    s0, s1, s2 = d2 - d1, d3 - d2, d4 - d3
    fix = correction(r_far * r_far, 6.0 * (r_mid * r_mid), r_near * r_near, s1 - s0, s2 - s1)
    return d2, d3, fix


def shifted_copies(gp, gm):
    return [roll(gp, k) for k in (2, 1, 0, -1, -2)] + [roll(gm, k) for k in (-3, -2, -1, 0, 1)]


def lane_faces(copies):
    low, high, fix_p = one_side(*copies[:5])
    back, front, fix_m = one_side(*copies[5:])
    inner = (high + front) - (fix_p + fix_m)
    return 6.0 * (copies[2] + copies[7]) + (low + back) + 2.0 * inner


def exchange_groups(nx, ny):
    cores = 2 - nx % 2
    width = min(4, nx // cores)
    depth = nx // (cores * width)
    low = 2 - ny % 2
    length = ny // low
    plane, column = [], []
    for a in range(depth):
        for b in range(width):
            for c in range(low):
                far = min(b, width - b) + (2 if a else c)
                plane.append((far, (a, b, 0, 0, c)))
    for d in range(length):
        for e in range(cores):
            column.append((min(d, length - d) + 0.2 * e, (0, 0, e, d, 0)))
    sizes = (depth, width, cores, length, low)
    plane, column = (
        [x for x in sorted(group, key=lambda x: -x[0]) if any(x[1])] for group in (plane, column)
    )
    return sizes, plane, column


def primitives(rho, m1, m2, m3, energy, reactant):
    inverse = reciprocal(rho)
    v1, v2, v3 = m1 * inverse, m2 * inverse, m3 * inverse
    kinetic = 0.5 * (m1 * v1 + m2 * v2 + m3 * v3)
    return v1, v2, v3, 0.4 * (energy - kinetic - reactant)


def signal_speed(rho, m1, m2, m3, energy, reactant):
    press = primitives(rho, m1, m2, m3, energy, reactant)[3]
    inverse = reciprocal(rho)
    fastest = jnp.maximum(jnp.maximum(jnp.abs(m1), jnp.abs(m2)), jnp.abs(m3))
    return fastest * inverse + jnp.sqrt(1.4 * press * inverse)


def kernel(
    nx, ny, state, inflow, out,
    raw, infl, turned, fields, prim, halo_prim, lined, acc, faces,
    windows, edges, ninth_p, ninth_m, ninth_d, ninth_out, ninth_in, ninth_halo, pack, opening,
    ends_out, ends_in, halo, peaks, consts,
    local_sem, send_sem, recv_sem,
):
    me_x, me_y = lax.axis_index("gx"), lax.axis_index("gy")
    is_first, is_last = me_x == 0, me_x == nx - 1
    lane = lax.broadcasted_iota(jnp.int32, (8, LANES), 1)
    sub = lax.broadcasted_iota(jnp.int32, (8, LANES), 0)
    place = lane & 15

    sizes, plane, column = exchange_groups(nx, ny)
    _, n_x, n_core, _, n_low = sizes
    digits = (
        me_x // (n_x * n_core), (me_x // n_core) % n_x, me_x % n_core, me_y // n_low, me_y % n_low
    )

    def peer(dx, dy):
        return (lax.rem(me_x + (dx + nx), nx), lax.rem(me_y + (dy + ny), ny))

    def partner(offset):
        a, b, c, d, e = (
            x if o == 0 else lax.rem(x + o, n) for x, o, n in zip(digits, offset, sizes)
        )
        return ((a * n_x + b) * n_core + c, d * n_low + e)

    def remote(src, dst, slot, target):
        return pltpu.make_async_remote_copy(
            src_ref=src, dst_ref=dst, send_sem=send_sem.at[slot], recv_sem=recv_sem.at[slot],
            device_id=target, device_id_type=MESH,
        )

    fetch_state = pltpu.make_async_copy(state, raw, local_sem.at[0])
    fetch_inflow = pltpu.make_async_copy(inflow, infl, local_sem.at[1])
    fetch_state.start()
    fetch_inflow.start()
    barrier = pltpu.get_barrier_semaphore()
    greeted = [partner(offset) for _, offset in sorted(plane + column, key=lambda x: -x[0])]
    greeted += [peer(1, 0), peer(-1, 0), peer(0, 1), peer(0, -1)]
    for device in greeted:
        pl.semaphore_signal(barrier, inc=1, device_id=device, device_id_type=MESH)
    fetch_state.wait()
    fetch_inflow.wait()

    def tile_speed(ref, tile, stride):
        rows = [ref[pl.ds(stride * c + 8 * tile, 8), :] for c in range(6)]
        return signal_speed(*rows)

    peak = tile_speed(raw, 0, 64)
    for g in range(1, GROUPS):
        peak = jnp.maximum(peak, tile_speed(raw, g, 64))
    entering = tile_speed(infl, 0, 32)
    for z in range(1, NZ):
        entering = jnp.maximum(entering, tile_speed(infl, z, 32))
    peak = jnp.where(is_first & (lane < 8), 0.0, peak)
    top = jnp.maximum(jnp.max(peak), jnp.max(entering))
    peaks[0, 0:1, :] = jnp.full((1, LANES), top, jnp.float32)

    pl.semaphore_wait(barrier, len(greeted))

    def phase_copy(phase, rows, device):
        return remote(
            peaks.at[phase, pl.ds(0, rows)], peaks.at[phase, pl.ds(1, rows)], phase, device
        )

    def send_peak(phase, group):
        for k, (_, offset) in enumerate(group):
            remote(
                peaks.at[phase, pl.ds(0, 1)], peaks.at[phase, pl.ds(k + 1, 1)], phase, partner(offset)
            ).start()

    def largest(phase, group):
        phase_copy(phase, len(group), partner(group[0][1])).wait_recv()
        return jnp.max(peaks[phase, pl.ds(0, len(group) + 1), :], axis=0, keepdims=True)

    send_peak(0, plane)

    def opening_block(g, q):
        if q == 8:
            return raw[pl.ds(64 * 8 + 8 * g, 8), :]
        return raw[pl.ds(8 * g + q, 8, stride=64), :]

    for q in range(BLOCKS):
        head = jnp.zeros((8, LANES), jnp.float32)
        own = head
        for g in range(GROUPS):
            block = opening_block(g, q)
            here = (lane >> 4) == g
            head = jnp.where(here, roll(block, 16 * g + 5), head)
            own = jnp.where(here, roll(block, 16 * g - 5), own)
        pack[0, pl.ds(8 * q, 8), :] = head
        windows[pl.ds(8 * q, 8), :] = own

    shift_copy = remote(pack.at[0, pl.ds(0, 72)], opening, 2, peer(-1, 0))

    @pl.when(me_x > 0)
    def _():
        shift_copy.start()

    @pl.when(is_last)
    def _():
        for c in range(COMPS):
            turned[pl.ds(16 * c, 16), 0:32] = infl[pl.ds(32 * c, 32), :].T
        for q in range(BLOCKS):
            head = jnp.zeros((8, LANES), jnp.float32)
            for g in range(GROUPS):
                z, t = g // 2, g % 2
                rows = pl.ds(8 * t + q, 8, stride=16) if q < 8 else pl.ds(128 + 8 * t, 8)
                block = roll(turned[rows, :], 16 * g + 5 - 8 * z)
                head = jnp.where((lane >> 4) == g, block, head)
            for k in range(1, 4):
                head = jnp.where(place == 12 + k, roll(head, k), head)
            opening[pl.ds(8 * q, 8), :] = head

    peaks[1, 0:1, :] = largest(0, plane)
    send_peak(1, column)

    @pl.when(jnp.logical_not(is_last))
    def _():
        shift_copy.wait_recv()

    for q in range(BLOCKS):
        rows = pl.ds(8 * q, 8)
        arrived = opening[rows, :]
        for g in range(GROUPS):
            block = opening_block(g, q)
            block = jnp.where(lane < LANES - 8, roll(block, -8), roll(arrived, 115 - 16 * g))
            fields[0, g // 2, g % 2, rows, :] = block
        own = windows[rows, :]
        edge = own
        for k in range(1, 4):
            edge = jnp.where(place == 3 - k, roll(own, -k), edge)
        own = jnp.where(is_first, edge, own)
        windows[rows, :] = jnp.where(place < 8, own, arrived)

    def pack_ninth(stage):
        for z in range(NZ):
            ninth_out[stage, 0, 4 * z : 4 * z + 3, :] = fields[stage, z, 1, 69:72, :]
            ninth_out[stage, 1, 4 * z : 4 * z + 3, :] = fields[stage, z, 0, 64:67, :]

    def y_copies(stage):
        now, base = fields.at[stage], 3 + 4 * stage
        up, down = peer(0, 1), peer(0, -1)
        return [
            remote(now.at[:, 1, 40:64, :], halo.at[stage, 0], base, up),
            remote(now.at[:, 0, 0:24, :], halo.at[stage, 1], base + 1, down),
            remote(ninth_out.at[stage, 0], ninth_in.at[stage, 0], base + 2, up),
            remote(ninth_out.at[stage, 1], ninth_in.at[stage, 1], base + 3, down),
        ]

    def x_copies(stage):
        base = 15 + 2 * (stage - 1)
        return [
            remote(ends_out.at[stage - 1, 0], ends_in.at[stage - 1, 0], base, peer(1, 0)),
            remote(ends_out.at[stage - 1, 1], ends_in.at[stage - 1, 1], base + 1, peer(-1, 0)),
        ]

    pack_ninth(0)
    for copy in y_copies(0):
        copy.start()

    def fluxes(block, velocity, press, lam, component):
        flow = velocity * (block + jnp.where(sub == 4, press, 0.0))
        flow = flow + jnp.where(sub == component, press, 0.0)
        move = lam * block
        return flow + move, flow - move

    def ninth_fluxes(block, velocity, lam):
        flow, move = velocity * block, lam * block
        return flow + move, flow - move

    for stage in range(3):
        now = fields.at[stage]
        for g in range(GROUPS):
            rows = [now[g // 2, g % 2, pl.ds(c, 8, stride=8), :] for c in range(6)]
            for index, value in enumerate(primitives(*rows)):
                prim[index, g] = value

        if stage == 0:
            speed = jnp.broadcast_to(largest(1, column), (8, LANES))
            consts[0] = speed
            consts[1] = COURANT / speed
        lam = consts[0]

        def spanwise(t, _):
            for q in range(BLOCKS):
                rows = pl.ds(8 * q, 8)
                gp, gm = [], []
                for z in range(NZ):
                    block = now[z, t, rows, :]
                    if q < 8:
                        v1, v3, press = (prim[i, 2 * z + t, q : q + 1, :] for i in (0, 2, 3))
                        one = fluxes(block, v1, press, lam, 1)
                        three = fluxes(block, v3, press, lam, 3)
                    else:
                        one = ninth_fluxes(block, prim[0, 2 * z + t], lam)
                        three = ninth_fluxes(block, prim[2, 2 * z + t], lam)
                    for k, value in enumerate(shifted_copies(*one)):
                        lined[k, z, t, rows, :] = value
                    gp.append(three[0])
                    gm.append(three[1])
                for z, value in enumerate(ring_differences(gp, gm)):
                    acc[z, t, rows, :] = value
            return 0

        lax.fori_loop(0, 2, spanwise, 0)

        def streamwise(g, _):
            z, t = g // 2, g % 2
            for q in range(BLOCKS):
                rows = pl.ds(8 * q, 8)
                faces[z, t, rows, :] = lane_faces([lined[k, z, t, rows, :] for k in range(10)])
            return 0

        lax.fori_loop(0, GROUPS, streamwise, 0)

        if stage > 0:
            left, right = x_copies(stage)

            @pl.when(me_x > 0)
            def _():
                left.wait_recv()

            @pl.when(jnp.logical_not(is_last))
            def _():
                right.wait_recv()

            for q in range(BLOCKS):
                rows = pl.ds(8 * q, 8)
                own = pack[stage, rows, :]
                low, high = own, own
                for k in range(1, 4):
                    low = jnp.where(place == 3 - k, roll(own, -k), low)
                    high = jnp.where(place == 12 + k, roll(own, k), high)
                tile, at = pl.ds(8 * (q // 5), 8), 3 * (q % 5)
                low = jnp.where(is_first, low, roll(ends_in[stage - 1, 0, tile, :], -at))
                high = jnp.where(is_last, high, roll(ends_in[stage - 1, 1, tile, :], 13 - at))
                windows[rows, :] = jnp.where(place < 3, low, jnp.where(place > 12, high, own))

        rows6 = [windows[pl.ds(c, 8, stride=8), :] for c in range(6)]
        v1, _, _, press = primitives(*rows6)
        edges[0, pl.ds(0, 8), :] = v1
        edges[0, pl.ds(8, 8), :] = press
        for q in range(BLOCKS):
            rows = pl.ds(8 * q, 8)
            block = windows[rows, :]
            if q < 8:
                pair = fluxes(block, edges[0, q : q + 1, :], edges[0, 8 + q : 9 + q, :], lam, 1)
            else:
                pair = ninth_fluxes(block, v1, lam)
            face = lane_faces(shifted_copies(*pair))
            edges[1, rows, :] = jnp.where(place < 3, roll(face, -9), roll(face, 1))
            edges[2, rows, :] = jnp.where(place < 3, roll(face, -10), face)

        for copy in y_copies(stage):
            copy.wait_recv()
        for side in range(2):
            for z in range(NZ):
                rows = [halo[stage, side, z, pl.ds(c, 3, stride=8), :] for c in range(6)]
                _, v2, _, press = primitives(*rows)
                start = 5 if side == 0 else 0
                halo_prim[0, side, z, start : start + 3, :] = v2
                halo_prim[1, side, z, start : start + 3, :] = press
                ninth_halo[side, z, start : start + 3, :] = ninth_in[stage, side, 4 * z : 4 * z + 3, :]

        def streamwise_difference(z, t, q):
            rows = pl.ds(8 * q, 8)
            back = 125 - 32 * z - 16 * t
            face = faces[z, t, rows, :]
            under = jnp.where(
                (lane < 3) | (lane > 125), pltpu.roll(edges[1, rows, :], back, axis=1), roll(face, 1)
            )
            face = jnp.where(
                (lane < 2) | (lane > 124), pltpu.roll(edges[2, rows, :], back, axis=1), face
            )
            return face - under

        def transverse(z, _):
            def load(j):
                if 0 <= j < NY:
                    t, q = j // 8, j % 8
                    block = now[z, t, pl.ds(8 * q, 8), :]
                    v2, press = (prim[i, 2 * z + t, q : q + 1, :] for i in (1, 3))
                else:
                    side, q = (0, j + 8) if j < 0 else (1, j - NY)
                    block = halo[stage, side, z, pl.ds(8 * (j + 3 if j < 0 else q), 8), :]
                    v2, press = (halo_prim[i, side, z, q : q + 1, :] for i in (0, 1))
                return fluxes(block, v2, press, lam, 2)

            before = {}

            def emit(i, face):
                before[i] = face
                if i >= 0:
                    t, q = i // 8, i % 8
                    total = (face - before.pop(i - 1)) + streamwise_difference(z, t, q)
                    acc[z, t, pl.ds(8 * q, 8), :] += total

            stream_faces(load, -1, NY - 1, emit)
            for t in range(2):
                acc[z, t, pl.ds(64, 8), :] += streamwise_difference(z, t, 8)

            tiles = [
                (ninth_halo[0, z], halo_prim[0, 0, z]),
                (now[z, 0, pl.ds(64, 8), :], prim[1, 2 * z]),
                (now[z, 1, pl.ds(64, 8), :], prim[1, 2 * z + 1]),
                (ninth_halo[1, z], halo_prim[0, 1, z]),
            ]
            for index, (block, v2) in enumerate(tiles):
                plus, minus = ninth_fluxes(block, v2, lam)
                for h in range(2):
                    if 0 <= index - h < 3:
                        start = pl.multiple_of(24 * z + 96 * h + 8 * (index - h), 8)
                        ninth_p[pl.ds(start, 8), :] = plus
                        ninth_m[pl.ds(start, 8), :] = minus
            return 0

        lax.fori_loop(0, NZ, transverse, 0)

        before = {}

        def emit_ninth(i, face):
            before[i] = face
            if i >= 0:
                ninth_d[pl.ds(i, 8, stride=8), :] = face - before.pop(i - 1)

        def load_ninth(j):
            rows = pl.ds(8 + j, 8, stride=24)
            return ninth_p[rows, :], ninth_m[rows, :]

        stream_faces(load_ninth, -1, 7, emit_ninth)
        for h in range(2):
            for z in range(NZ):
                acc[z, h, pl.ds(64, 8), :] += ninth_d[pl.ds(8 * (4 * h + z), 8), :]

        keep, blend = STAGES[stage]

        scale = consts[1] * (blend / 12.0)

        def update(q, z, t):
            rows = pl.ds(8 * q, 8)
            value = now[z, t, rows, :]
            if stage > 0:
                value = keep * fields[0, z, t, rows, :] + blend * value
            value = value - scale * acc[z, t, rows, :]
            fields[stage + 1, z, t, rows, :] = value
            return value

        outer = [(0, 0), (1, 0), (2, 0), (8, 0), (5, 1), (6, 1), (7, 1), (8, 1)]
        for q, t in outer:
            for z in range(NZ):
                update(q, z, t)
        if stage < 2:
            pack_ninth(stage + 1)
            for copy in y_copies(stage + 1):
                copy.start()

        for q in range(BLOCKS):
            rows = pl.ds(8 * q, 8)
            packed = jnp.zeros((8, LANES), jnp.float32)
            for g in range(GROUPS):
                z, t = g // 2, g % 2
                value = fields[stage + 1, z, t, rows, :] if (q, t) in outer else update(q, z, t)
                if stage < 2:
                    here = (lane >> 4) == g
                    ends = jnp.where(place < 8, roll(value, 16 * g + 3), roll(value, 16 * g + 13))
                    packed = jnp.where(here, ends, packed)
            if stage < 2:
                pack[stage + 1, rows, :] = packed

        def pack_ends(tile, _):
            for side in range(2):
                joined = jnp.zeros((8, LANES), jnp.float32)
                for k in range(5):
                    window = pack[stage + 1, pl.ds(pl.multiple_of(40 * tile + 8 * k, 8), 8), :]
                    moved = roll(window, 3 * k - 13 * side)
                    joined = jnp.where((place >= 3 * k) & (place < 3 * k + 3), moved, joined)
                ends_out[stage, side, pl.ds(pl.multiple_of(8 * tile, 8), 8), :] = joined
            return 0

        if stage < 2:
            lax.fori_loop(0, 2, pack_ends, 0)
            left, right = x_copies(stage + 1)

            @pl.when(jnp.logical_not(is_last))
            def _():
                left.start()

            @pl.when(me_x > 0)
            def _():
                right.start()

    third = fields.at[3]

    for g in range(GROUPS):
        z, t = g // 2, g % 2
        rows = [third[z, t, pl.ds(c, 8, stride=8), :] for c in range(8)]
        rho, m1, m2, m3, energy, reactant, product, other = rows
        inverse = reciprocal(rho)
        rest = energy - 0.5 * (m1 * m1 + m2 * m2 + m3 * m3) * inverse
        small = consts[1] * (PREFACTOR / SUBSTEPS)
        for _ in range(SUBSTEPS):
            press = 0.4 * (rest - reactant)
            burned = small * reactant * jnp.exp(-ACTIVATION * (rho * reciprocal(press)))
            reactant, product = reactant - burned, product + burned
        rows = [rho, m1, m2, m3, energy, reactant, product, other, third[z, t, pl.ds(64, 8), :]]
        for c, value in enumerate(rows):
            out[pl.ds(64 * c + 8 * g, 8), :] = value

    for phase, group in enumerate((plane, column)):
        phase_copy(phase, len(group), partner(group[0][1])).wait_send()
    for copy in y_copies(0) + y_copies(1) + y_copies(2):
        copy.wait_send()
    for stage in (1, 2):
        left, right = x_copies(stage)

        @pl.when(jnp.logical_not(is_last))
        def _():
            left.wait_send()

        @pl.when(me_x > 0)
        def _():
            right.wait_send()

    @pl.when(me_x > 0)
    def _():
        shift_copy.wait_send()


def on_device(nx, ny, state, inflow):
    rows = COMPS * NZ * NY
    f32 = jnp.float32

    inflow = jnp.swapaxes(inflow, 2, 3).reshape(COMPS * NZ * inflow.shape[3], NY)

    def vmem(*shape):
        return pltpu.VMEM(shape, f32)

    result = pl.pallas_call(
        functools.partial(kernel, nx, ny),
        out_shape=jax.ShapeDtypeStruct((rows, LANES), f32),
        in_specs=[pl.BlockSpec(memory_space=pltpu.HBM)] * 2,
        out_specs=pl.BlockSpec(memory_space=pltpu.VMEM),
        scratch_shapes=[
            vmem(rows, LANES),
            vmem(*inflow.shape),
            vmem(COMPS * NY, LANES),
            vmem(4, NZ, 2, 72, LANES),
            vmem(4, GROUPS, 8, LANES),
            vmem(2, 2, NZ, 8, LANES),
            vmem(10, NZ, 2, 72, LANES),
            vmem(NZ, 2, 72, LANES),
            vmem(NZ, 2, 72, LANES),
            vmem(72, LANES),
            vmem(3, 72, LANES),
            vmem(192, LANES),
            vmem(192, LANES),
            vmem(64, LANES),
            vmem(3, 2, 16, LANES),
            vmem(3, 2, 16, LANES),
            vmem(2, NZ, 8, LANES),
            vmem(3, 80, LANES),
            vmem(72, LANES),
            vmem(2, 2, 16, LANES),
            vmem(2, 2, 16, LANES),
            vmem(3, 2, NZ, 24, LANES),
            vmem(2, 32, LANES),
            vmem(2, 8, LANES),
            pltpu.SemaphoreType.DMA((2,)),
            pltpu.SemaphoreType.DMA((20,)),
            pltpu.SemaphoreType.DMA((20,)),
        ],
        compiler_params=pltpu.CompilerParams(
            collective_id=0, has_side_effects=True, vmem_limit_bytes=54720 * 1024
        ),
        cost_estimate=pl.CostEstimate(
            flops=60_000_000, bytes_accessed=1_200_000, transcendentals=5_000_000
        ),
    )(state.reshape(rows, LANES), inflow)
    return result.reshape(state.shape)


def solution(mesh):
    return jax.shard_map(
        functools.partial(on_device, mesh.shape["gx"], mesh.shape["gy"]),
        mesh=mesh,
        in_specs=(P(None, None, "gy", "gx"), P(None, None, "gy", None)),
        out_specs=P(None, None, "gy", "gx"),
        check_vma=False,
    )
```

```python
import functools

import jax
import jax.numpy as jnp
from jax import lax
from jax.experimental import pallas as pl
from jax.experimental.pallas import tpu as pltpu
from jax.sharding import PartitionSpec as P

MESH = pl.DeviceIdType.MESH
NZ = 4
NY = 16
LANES = 128
COMPS = 9
GROUPS = 8
BLOCKS = 9
SUBSTEPS = 4
PREFACTOR = 300.0
ACTIVATION = 4.0
COURANT = 0.15
EPS = 2e-6
STAGES = ((0.0, 1.0), (0.75, 0.25), (1.0 / 3.0, 2.0 / 3.0))


def reciprocal(x):
    return pltpu.reciprocal(x, approx=True)


def roll(x, shift):
    shift = shift % LANES
    return x if shift == 0 else pltpu.roll(x, shift, axis=1)


def cell_terms(d_low, d_high, q_low, q_high):
    second = d_high - d_low
    half = d_low * (0.5 * d_high)
    level = (2.0 / 3.0) * (second * second) + EPS
    base = level - half
    r_low = reciprocal(base + q_high)
    r_mid = reciprocal(level + half)
    r_high = reciprocal(base + q_low)
    return second, r_low * r_low, 6.0 * (r_mid * r_mid), r_high * r_high


def correction(w_far, w_mid, w_near, t_far, t_near):
    near = 3.0 * w_near
    return (w_far * t_far + near * (0.5 * t_near)) * reciprocal((w_far + w_mid) + near)


def face_value(gp, gm, dp_low, dp_high, dm_low, dm_high, fix_p, fix_m):
    inner = (dp_high - dm_low) - (fix_p - fix_m)
    return 6.0 * (gp + gm) + (dp_low - dm_high) + 2.0 * inner


def stream_faces(load, first, last, emit):
    gp, gm, dp, dm, qp, qm = {}, {}, {}, {}, {}, {}
    tp, tm, sp, sm, wp, wm = {}, {}, {}, {}, {}, {}
    fix = {}
    for j in range(first - 2, last + 4):
        gp[j], gm[j] = load(j)
        k = j - 1
        if j > first - 2:
            dp[k] = gp[j] - gp[k]
            qp[k] = dp[k] * dp[k]
            dm[k] = gm[j] - gm[k]
            qm[k] = dm[k] * dm[k]
        if j >= first:
            sp[k], *wp[k] = cell_terms(dp[k - 1], dp[k], qp[k - 1], qp[k])
            sm[k], *wm[k] = cell_terms(dm[k - 1], dm[k], qm[k - 1], qm[k])
            if k > first - 1:
                tp[k - 1] = sp[k] - sp[k - 1]
                tm[k - 1] = sm[k] - sm[k - 1]
            i = k - 1
            if first <= i <= last:
                fix[i] = correction(wp[i - 1][0], wp[i][1], wp[i + 1][2], tp[i - 1], tp[i])
            i, c = k - 2, k - 1
            if first <= i <= last:
                fix_m = correction(wm[c + 1][2], wm[c][1], wm[c - 1][0], tm[c], tm[c - 1])
                emit(i, face_value(gp[i], gm[c], dp[i - 1], dp[i], dm[i], dm[c], fix[i], fix_m))


def ring_differences(gp, gm):
    n = len(gp)

    def up(x):
        return [x[(i + 1) % n] for i in range(n)]

    def down(x):
        return [x[(i - 1) % n] for i in range(n)]

    def parts(g):
        d = [b - a for a, b in zip(g, up(g))]
        q = [a * a for a in d]
        terms = [cell_terms(*each) for each in zip(down(d), d, down(q), q)]
        s, low, mid, high = map(list, zip(*terms))
        t = [b - a for a, b in zip(s, up(s))]
        return d, t, low, mid, high

    dp, t, low, mid, high = parts(gp)
    fix_p = [correction(*each) for each in zip(down(low), mid, up(high), down(t), t)]
    dm, t, low, mid, high = parts(gm)
    fix_m = [correction(*each) for each in zip(up(high), mid, down(low), t, down(t))]
    faces = [
        face_value(*each) for each in zip(gp, up(gm), down(dp), dp, dm, up(dm), fix_p, up(fix_m))
    ]
    return [a - b for a, b in zip(faces, down(faces))]


def one_side(far, near, centre, ahead, beyond):
    d1, d2, d3, d4 = near - far, centre - near, ahead - centre, beyond - ahead
    q2, q3 = d2 * d2, d3 * d3
    r_far = reciprocal(d1 * (d1 - 2.75 * d2) + (2.5 * q2 + 1.5 * EPS))
    r_mid = reciprocal(d2 * (d2 - 1.25 * d3) + (q3 + 1.5 * EPS))
    r_near = reciprocal(d4 * (d4 - 2.75 * d3) + (2.5 * q3 + 1.5 * EPS))
    s0, s1, s2 = d2 - d1, d3 - d2, d4 - d3
    fix = correction(r_far * r_far, 6.0 * (r_mid * r_mid), r_near * r_near, s1 - s0, s2 - s1)
    return d2, d3, fix


def shifted_copies(gp, gm):
    return [roll(gp, k) for k in (2, 1, 0, -1, -2)] + [roll(gm, k) for k in (-3, -2, -1, 0, 1)]


def lane_faces(copies):
    low, high, fix_p = one_side(*copies[:5])
    back, front, fix_m = one_side(*copies[5:])
    inner = (high + front) - (fix_p + fix_m)
    return 6.0 * (copies[2] + copies[7]) + (low + back) + 2.0 * inner


def exchange_groups(nx, ny):
    cores = 2 - nx % 2
    width = min(4, nx // cores)
    depth = nx // (cores * width)
    low = 2 - ny % 2
    length = ny // low
    plane, column = [], []
    for a in range(depth):
        for b in range(width):
            for c in range(low):
                far = min(b, width - b) + (2 if a else c)
                plane.append((far, (a, b, 0, 0, c)))
    for d in range(length):
        for e in range(cores):
            column.append((min(d, length - d) + 0.2 * e, (0, 0, e, d, 0)))
    sizes = (depth, width, cores, length, low)
    plane, column = (
        [x for x in sorted(group, key=lambda x: -x[0]) if any(x[1])] for group in (plane, column)
    )
    return sizes, plane, column


def primitives(rho, m1, m2, m3, energy, reactant):
    inverse = reciprocal(rho)
    v1, v2, v3 = m1 * inverse, m2 * inverse, m3 * inverse
    kinetic = 0.5 * (m1 * v1 + m2 * v2 + m3 * v3)
    return v1, v2, v3, 0.4 * (energy - kinetic - reactant)


def signal_speed(rho, m1, m2, m3, energy, reactant):
    press = primitives(rho, m1, m2, m3, energy, reactant)[3]
    inverse = reciprocal(rho)
    fastest = jnp.maximum(jnp.maximum(jnp.abs(m1), jnp.abs(m2)), jnp.abs(m3))
    return fastest * inverse + jnp.sqrt(1.4 * press * inverse)


def kernel(
    nx, ny, state, inflow, out,
    raw, infl, turned, fields, prim, halo_prim, lined, acc, faces,
    windows, edges, ninth_p, ninth_m, ninth_d, ninth_out, ninth_in, ninth_halo, pack, opening,
    ends_out, ends_in, halo, peaks, consts,
    local_sem, send_sem, recv_sem,
):
    me_x, me_y = lax.axis_index("gx"), lax.axis_index("gy")
    is_first, is_last = me_x == 0, me_x == nx - 1
    lane = lax.broadcasted_iota(jnp.int32, (8, LANES), 1)
    sub = lax.broadcasted_iota(jnp.int32, (8, LANES), 0)
    place = lane & 15

    sizes, plane, column = exchange_groups(nx, ny)
    _, n_x, n_core, _, n_low = sizes
    digits = (
        me_x // (n_x * n_core), (me_x // n_core) % n_x, me_x % n_core, me_y // n_low, me_y % n_low
    )

    def peer(dx, dy):
        return (lax.rem(me_x + (dx + nx), nx), lax.rem(me_y + (dy + ny), ny))

    def partner(offset):
        a, b, c, d, e = (
            x if o == 0 else lax.rem(x + o, n) for x, o, n in zip(digits, offset, sizes)
        )
        return ((a * n_x + b) * n_core + c, d * n_low + e)

    def remote(src, dst, slot, target):
        return pltpu.make_async_remote_copy(
            src_ref=src, dst_ref=dst, send_sem=send_sem.at[slot], recv_sem=recv_sem.at[slot],
            device_id=target, device_id_type=MESH,
        )

    fetch_state = pltpu.make_async_copy(state, raw, local_sem.at[0])
    fetch_inflow = pltpu.make_async_copy(inflow, infl, local_sem.at[1])
    fetch_state.start()
    fetch_inflow.start()
    barrier = pltpu.get_barrier_semaphore()
    greeted = [partner(offset) for _, offset in sorted(plane + column, key=lambda x: -x[0])]
    greeted += [peer(1, 0), peer(-1, 0), peer(0, 1), peer(0, -1)]
    for device in greeted:
        pl.semaphore_signal(barrier, inc=1, device_id=device, device_id_type=MESH)
    fetch_state.wait()
    fetch_inflow.wait()

    def tile_speed(ref, tile, stride):
        rows = [ref[pl.ds(stride * c + 8 * tile, 8), :] for c in range(6)]
        return signal_speed(*rows)

    peak = tile_speed(raw, 0, 64)
    for g in range(1, GROUPS):
        peak = jnp.maximum(peak, tile_speed(raw, g, 64))
    entering = tile_speed(infl, 0, 32)
    for z in range(1, NZ):
        entering = jnp.maximum(entering, tile_speed(infl, z, 32))
    peak = jnp.where(is_first & (lane < 8), 0.0, peak)
    top = jnp.maximum(jnp.max(peak), jnp.max(entering))
    peaks[0, 0:1, :] = jnp.full((1, LANES), top, jnp.float32)

    pl.semaphore_wait(barrier, len(greeted))

    def phase_copy(phase, rows, device):
        return remote(
            peaks.at[phase, pl.ds(0, rows)], peaks.at[phase, pl.ds(1, rows)], phase, device
        )

    def send_peak(phase, group):
        for k, (_, offset) in enumerate(group):
            remote(
                peaks.at[phase, pl.ds(0, 1)], peaks.at[phase, pl.ds(k + 1, 1)], phase, partner(offset)
            ).start()

    def largest(phase, group):
        phase_copy(phase, len(group), partner(group[0][1])).wait_recv()
        return jnp.max(peaks[phase, pl.ds(0, len(group) + 1), :], axis=0, keepdims=True)

    send_peak(0, plane)

    def opening_block(g, q):
        if q == 8:
            return raw[pl.ds(64 * 8 + 8 * g, 8), :]
        return raw[pl.ds(8 * g + q, 8, stride=64), :]

    for q in range(BLOCKS):
        head = jnp.zeros((8, LANES), jnp.float32)
        own = head
        for g in range(GROUPS):
            block = opening_block(g, q)
            here = (lane >> 4) == g
            head = jnp.where(here, roll(block, 16 * g + 5), head)
            own = jnp.where(here, roll(block, 16 * g - 5), own)
        pack[0, pl.ds(8 * q, 8), :] = head
        windows[pl.ds(8 * q, 8), :] = own

    shift_copy = remote(pack.at[0, pl.ds(0, 72)], opening, 2, peer(-1, 0))

    @pl.when(me_x > 0)
    def _():
        shift_copy.start()

    @pl.when(is_last)
    def _():
        for c in range(COMPS):
            turned[pl.ds(16 * c, 16), 0:32] = infl[pl.ds(32 * c, 32), :].T
        for q in range(BLOCKS):
            head = jnp.zeros((8, LANES), jnp.float32)
            for g in range(GROUPS):
                z, t = g // 2, g % 2
                rows = pl.ds(8 * t + q, 8, stride=16) if q < 8 else pl.ds(128 + 8 * t, 8)
                block = roll(turned[rows, :], 16 * g + 5 - 8 * z)
                head = jnp.where((lane >> 4) == g, block, head)
            for k in range(1, 4):
                head = jnp.where(place == 12 + k, roll(head, k), head)
            opening[pl.ds(8 * q, 8), :] = head

    peaks[1, 0:1, :] = largest(0, plane)
    send_peak(1, column)

    @pl.when(jnp.logical_not(is_last))
    def _():
        shift_copy.wait_recv()

    for q in range(BLOCKS):
        rows = pl.ds(8 * q, 8)
        arrived = opening[rows, :]
        for g in range(GROUPS):
            block = opening_block(g, q)
            block = jnp.where(lane < LANES - 8, roll(block, -8), roll(arrived, 115 - 16 * g))
            fields[0, g // 2, g % 2, rows, :] = block
        own = windows[rows, :]
        edge = own
        for k in range(1, 4):
            edge = jnp.where(place == 3 - k, roll(own, -k), edge)
        own = jnp.where(is_first, edge, own)
        windows[rows, :] = jnp.where(place < 8, own, arrived)

    def pack_ninth(stage):
        for z in range(NZ):
            ninth_out[stage, 0, 4 * z : 4 * z + 3, :] = fields[stage, z, 1, 69:72, :]
            ninth_out[stage, 1, 4 * z : 4 * z + 3, :] = fields[stage, z, 0, 64:67, :]

    def y_copies(stage):
        now, base = fields.at[stage], 3 + 4 * stage
        up, down = peer(0, 1), peer(0, -1)
        return [
            remote(now.at[:, 1, 40:64, :], halo.at[stage, 0], base, up),
            remote(now.at[:, 0, 0:24, :], halo.at[stage, 1], base + 1, down),
            remote(ninth_out.at[stage, 0], ninth_in.at[stage, 0], base + 2, up),
            remote(ninth_out.at[stage, 1], ninth_in.at[stage, 1], base + 3, down),
        ]

    def x_copies(stage):
        base = 15 + 2 * (stage - 1)
        return [
            remote(ends_out.at[stage - 1, 0], ends_in.at[stage - 1, 0], base, peer(1, 0)),
            remote(ends_out.at[stage - 1, 1], ends_in.at[stage - 1, 1], base + 1, peer(-1, 0)),
        ]

    pack_ninth(0)
    for copy in y_copies(0):
        copy.start()

    def fluxes(block, velocity, press, lam, component):
        flow = velocity * (block + jnp.where(sub == 4, press, 0.0))
        flow = flow + jnp.where(sub == component, press, 0.0)
        move = lam * block
        return flow + move, flow - move

    def ninth_fluxes(block, velocity, lam):
        flow, move = velocity * block, lam * block
        return flow + move, flow - move

    for stage in range(3):
        now = fields.at[stage]
        for g in range(GROUPS):
            rows = [now[g // 2, g % 2, pl.ds(c, 8, stride=8), :] for c in range(6)]
            for index, value in enumerate(primitives(*rows)):
                prim[index, g] = value

        if stage == 0:
            speed = jnp.broadcast_to(largest(1, column), (8, LANES))
            consts[0] = speed
            consts[1] = COURANT / speed
        lam = consts[0]

        def spanwise(t, _):
            for q in range(BLOCKS):
                rows = pl.ds(8 * q, 8)
                gp, gm = [], []
                for z in range(NZ):
                    block = now[z, t, rows, :]
                    if q < 8:
                        v1, v3, press = (prim[i, 2 * z + t, q : q + 1, :] for i in (0, 2, 3))
                        one = fluxes(block, v1, press, lam, 1)
                        three = fluxes(block, v3, press, lam, 3)
                    else:
                        one = ninth_fluxes(block, prim[0, 2 * z + t], lam)
                        three = ninth_fluxes(block, prim[2, 2 * z + t], lam)
                    for k, value in enumerate(shifted_copies(*one)):
                        lined[k, z, t, rows, :] = value
                    gp.append(three[0])
                    gm.append(three[1])
                for z, value in enumerate(ring_differences(gp, gm)):
                    acc[z, t, rows, :] = value
            return 0

        lax.fori_loop(0, 2, spanwise, 0)

        def streamwise(g, _):
            z, t = g // 2, g % 2
            for q in range(BLOCKS):
                rows = pl.ds(8 * q, 8)
                faces[z, t, rows, :] = lane_faces([lined[k, z, t, rows, :] for k in range(10)])
            return 0

        lax.fori_loop(0, GROUPS, streamwise, 0)

        if stage > 0:
            left, right = x_copies(stage)

            @pl.when(me_x > 0)
            def _():
                left.wait_recv()

            @pl.when(jnp.logical_not(is_last))
            def _():
                right.wait_recv()

            for q in range(BLOCKS):
                rows = pl.ds(8 * q, 8)
                own = pack[stage, rows, :]
                low, high = own, own
                for k in range(1, 4):
                    low = jnp.where(place == 3 - k, roll(own, -k), low)
                    high = jnp.where(place == 12 + k, roll(own, k), high)
                tile, at = pl.ds(8 * (q // 5), 8), 3 * (q % 5)
                low = jnp.where(is_first, low, roll(ends_in[stage - 1, 0, tile, :], -at))
                high = jnp.where(is_last, high, roll(ends_in[stage - 1, 1, tile, :], 13 - at))
                windows[rows, :] = jnp.where(place < 3, low, jnp.where(place > 12, high, own))

        rows6 = [windows[pl.ds(c, 8, stride=8), :] for c in range(6)]
        v1, _, _, press = primitives(*rows6)
        edges[0, pl.ds(0, 8), :] = v1
        edges[0, pl.ds(8, 8), :] = press
        for q in range(BLOCKS):
            rows = pl.ds(8 * q, 8)
            block = windows[rows, :]
            if q < 8:
                pair = fluxes(block, edges[0, q : q + 1, :], edges[0, 8 + q : 9 + q, :], lam, 1)
            else:
                pair = ninth_fluxes(block, v1, lam)
            face = lane_faces(shifted_copies(*pair))
            edges[1, rows, :] = jnp.where(place < 3, roll(face, -9), roll(face, 1))
            edges[2, rows, :] = jnp.where(place < 3, roll(face, -10), face)

        if stage == 2:
            for phase, group in enumerate((plane, column)):
                phase_copy(phase, len(group), partner(group[0][1])).wait_send()
            for copy in y_copies(0) + y_copies(1) + y_copies(2):
                copy.wait_send()
            for later in (1, 2):
                left, right = x_copies(later)

                @pl.when(jnp.logical_not(is_last))
                def _():
                    left.wait_send()

                @pl.when(me_x > 0)
                def _():
                    right.wait_send()

            @pl.when(me_x > 0)
            def _():
                shift_copy.wait_send()

        for copy in y_copies(stage):
            copy.wait_recv()
        for side in range(2):
            for z in range(NZ):
                rows = [halo[stage, side, z, pl.ds(c, 3, stride=8), :] for c in range(6)]
                _, v2, _, press = primitives(*rows)
                start = 5 if side == 0 else 0
                halo_prim[0, side, z, start : start + 3, :] = v2
                halo_prim[1, side, z, start : start + 3, :] = press
                ninth_halo[side, z, start : start + 3, :] = ninth_in[stage, side, 4 * z : 4 * z + 3, :]

        def streamwise_difference(z, t, q):
            rows = pl.ds(8 * q, 8)
            back = 125 - 32 * z - 16 * t
            face = faces[z, t, rows, :]
            under = jnp.where(
                (lane < 3) | (lane > 125), pltpu.roll(edges[1, rows, :], back, axis=1), roll(face, 1)
            )
            face = jnp.where(
                (lane < 2) | (lane > 124), pltpu.roll(edges[2, rows, :], back, axis=1), face
            )
            return face - under

        def transverse(z, _):
            def load(j):
                if 0 <= j < NY:
                    t, q = j // 8, j % 8
                    block = now[z, t, pl.ds(8 * q, 8), :]
                    v2, press = (prim[i, 2 * z + t, q : q + 1, :] for i in (1, 3))
                else:
                    side, q = (0, j + 8) if j < 0 else (1, j - NY)
                    block = halo[stage, side, z, pl.ds(8 * (j + 3 if j < 0 else q), 8), :]
                    v2, press = (halo_prim[i, side, z, q : q + 1, :] for i in (0, 1))
                return fluxes(block, v2, press, lam, 2)

            before = {}

            def emit(i, face):
                before[i] = face
                if i >= 0:
                    t, q = i // 8, i % 8
                    total = (face - before.pop(i - 1)) + streamwise_difference(z, t, q)
                    acc[z, t, pl.ds(8 * q, 8), :] += total

            stream_faces(load, -1, NY - 1, emit)
            for t in range(2):
                acc[z, t, pl.ds(64, 8), :] += streamwise_difference(z, t, 8)

            tiles = [
                (ninth_halo[0, z], halo_prim[0, 0, z]),
                (now[z, 0, pl.ds(64, 8), :], prim[1, 2 * z]),
                (now[z, 1, pl.ds(64, 8), :], prim[1, 2 * z + 1]),
                (ninth_halo[1, z], halo_prim[0, 1, z]),
            ]
            for index, (block, v2) in enumerate(tiles):
                plus, minus = ninth_fluxes(block, v2, lam)
                for h in range(2):
                    if 0 <= index - h < 3:
                        start = pl.multiple_of(24 * z + 96 * h + 8 * (index - h), 8)
                        ninth_p[pl.ds(start, 8), :] = plus
                        ninth_m[pl.ds(start, 8), :] = minus
            return 0

        lax.fori_loop(0, NZ, transverse, 0)

        before = {}

        def emit_ninth(i, face):
            before[i] = face
            if i >= 0:
                ninth_d[pl.ds(i, 8, stride=8), :] = face - before.pop(i - 1)

        def load_ninth(j):
            rows = pl.ds(8 + j, 8, stride=24)
            return ninth_p[rows, :], ninth_m[rows, :]

        stream_faces(load_ninth, -1, 7, emit_ninth)
        for h in range(2):
            for z in range(NZ):
                acc[z, h, pl.ds(64, 8), :] += ninth_d[pl.ds(8 * (4 * h + z), 8), :]

        keep, blend = STAGES[stage]

        scale = consts[1] * (blend / 12.0)

        def update(q, z, t):
            rows = pl.ds(8 * q, 8)
            value = now[z, t, rows, :]
            if stage > 0:
                value = keep * fields[0, z, t, rows, :] + blend * value
            value = value - scale * acc[z, t, rows, :]
            fields[stage + 1, z, t, rows, :] = value
            return value

        outer = [(0, 0), (1, 0), (2, 0), (8, 0), (5, 1), (6, 1), (7, 1), (8, 1)]
        for q, t in outer:
            for z in range(NZ):
                update(q, z, t)
        if stage < 2:
            pack_ninth(stage + 1)
            for copy in y_copies(stage + 1):
                copy.start()

        for q in range(BLOCKS):
            rows = pl.ds(8 * q, 8)
            packed = jnp.zeros((8, LANES), jnp.float32)
            for g in range(GROUPS):
                z, t = g // 2, g % 2
                value = fields[stage + 1, z, t, rows, :] if (q, t) in outer else update(q, z, t)
                if stage < 2:
                    here = (lane >> 4) == g
                    ends = jnp.where(place < 8, roll(value, 16 * g + 3), roll(value, 16 * g + 13))
                    packed = jnp.where(here, ends, packed)
            if stage < 2:
                pack[stage + 1, rows, :] = packed

        def pack_ends(tile, _):
            for side in range(2):
                joined = jnp.zeros((8, LANES), jnp.float32)
                for k in range(5):
                    window = pack[stage + 1, pl.ds(pl.multiple_of(40 * tile + 8 * k, 8), 8), :]
                    moved = roll(window, 3 * k - 13 * side)
                    joined = jnp.where((place >= 3 * k) & (place < 3 * k + 3), moved, joined)
                ends_out[stage, side, pl.ds(pl.multiple_of(8 * tile, 8), 8), :] = joined
            return 0

        if stage < 2:
            lax.fori_loop(0, 2, pack_ends, 0)
            left, right = x_copies(stage + 1)

            @pl.when(jnp.logical_not(is_last))
            def _():
                left.start()

            @pl.when(me_x > 0)
            def _():
                right.start()

    third = fields.at[3]

    for g in range(GROUPS):
        z, t = g // 2, g % 2
        rows = [third[z, t, pl.ds(c, 8, stride=8), :] for c in range(8)]
        rho, m1, m2, m3, energy, reactant, product, other = rows
        inverse = reciprocal(rho)
        rest = energy - 0.5 * (m1 * m1 + m2 * m2 + m3 * m3) * inverse
        small = consts[1] * (PREFACTOR / SUBSTEPS)
        for _ in range(SUBSTEPS):
            press = 0.4 * (rest - reactant)
            burned = small * reactant * jnp.exp(-ACTIVATION * (rho * reciprocal(press)))
            reactant, product = reactant - burned, product + burned
        rows = [rho, m1, m2, m3, energy, reactant, product, other, third[z, t, pl.ds(64, 8), :]]
        for c, value in enumerate(rows):
            out[pl.ds(64 * c + 8 * g, 8), :] = value


def on_device(nx, ny, state, inflow):
    rows = COMPS * NZ * NY
    f32 = jnp.float32

    inflow = jnp.swapaxes(inflow, 2, 3).reshape(COMPS * NZ * inflow.shape[3], NY)

    def vmem(*shape):
        return pltpu.VMEM(shape, f32)

    result = pl.pallas_call(
        functools.partial(kernel, nx, ny),
        out_shape=jax.ShapeDtypeStruct((rows, LANES), f32),
        in_specs=[pl.BlockSpec(memory_space=pltpu.HBM)] * 2,
        out_specs=pl.BlockSpec(memory_space=pltpu.VMEM),
        scratch_shapes=[
            vmem(rows, LANES),
            vmem(*inflow.shape),
            vmem(COMPS * NY, LANES),
            vmem(4, NZ, 2, 72, LANES),
            vmem(4, GROUPS, 8, LANES),
            vmem(2, 2, NZ, 8, LANES),
            vmem(10, NZ, 2, 72, LANES),
            vmem(NZ, 2, 72, LANES),
            vmem(NZ, 2, 72, LANES),
            vmem(72, LANES),
            vmem(3, 72, LANES),
            vmem(192, LANES),
            vmem(192, LANES),
            vmem(64, LANES),
            vmem(3, 2, 16, LANES),
            vmem(3, 2, 16, LANES),
            vmem(2, NZ, 8, LANES),
            vmem(3, 80, LANES),
            vmem(72, LANES),
            vmem(2, 2, 16, LANES),
            vmem(2, 2, 16, LANES),
            vmem(3, 2, NZ, 24, LANES),
            vmem(2, 32, LANES),
            vmem(2, 8, LANES),
            pltpu.SemaphoreType.DMA((2,)),
            pltpu.SemaphoreType.DMA((20,)),
            pltpu.SemaphoreType.DMA((20,)),
        ],
        compiler_params=pltpu.CompilerParams(
            collective_id=0, has_side_effects=True, vmem_limit_bytes=54720 * 1024
        ),
        cost_estimate=pl.CostEstimate(
            flops=60_000_000, bytes_accessed=1_200_000, transcendentals=5_000_000
        ),
    )(state.reshape(rows, LANES), inflow)
    return result.reshape(state.shape)


def solution(mesh):
    return jax.shard_map(
        functools.partial(on_device, mesh.shape["gx"], mesh.shape["gy"]),
        mesh=mesh,
        in_specs=(P(None, None, "gy", "gx"), P(None, None, "gy", None)),
        out_specs=P(None, None, "gy", "gx"),
        check_vma=False,
    )
```
